128 devices in a mesh: pipe: 4 (over z_hi, core), expert: 32 (over y, z_lo, x).
Axes of the slice: x: 4, y: 4, z: 4 (z_hi: 2, z_lo: 2; z = z_hi * 2 + z_lo), core: 2. Of those that a mesh axis runs over, the one named last changes fastest.
Arguments:
- fwd_src: bfloat16 [4, 2048, 7168], P('pipe', 'expert'), may hold values from -12.65 to 12.65
- fwd_route: int32 [4, 2048, 1], P('pipe', 'expert'), may hold values from 0 to 7, as said below
- bwd_input: bfloat16 [4, 2048, 7168], P('pipe', 'expert'), may hold values from -12.65 to 12.65
- bwd_expert_out: bfloat16 [4, 2048, 7168], P('pipe', 'expert'), may hold values from -4 to 4
- grad_src: bfloat16 [4, 2048, 7168], P('pipe', 'expert'), may hold values from -5 to 5
- bwd_route: int32 [4, 2048, 1], P('pipe', 'expert'), may hold values from 0 to 7, as said below
- norm_gain: bfloat16 [4, 7168], P('pipe'), may hold values from 0.099609375 to 1.8984375
- router: bfloat16 [4, 7168, 8], P('pipe'), may hold values from -0.0625 to 0.0625
- gate_w: bfloat16 [4, 7168, 8192], P('pipe', None, 'expert'), may hold values from -0.0625 to 0.0625
- up_w: bfloat16 [4, 7168, 8192], P('pipe', None, 'expert'), may hold values from -0.0625 to 0.0625
- down_w: bfloat16 [4, 8192, 7168], P('pipe', 'expert'), may hold values from -0.1875 to 0.1875
Outputs:
- fwd_out: bfloat16 [4, 2048, 7168], P('pipe', 'expert')
- bwd_out: bfloat16 [4, 2048, 7168], P('pipe', 'expert')
The draws below stay inside these ranges and needn't reach their ends.
Inputs may be any that keep to these rules, and one draw needn't show every extreme that they name: `fwd_route`: at every section one expert, drawn from the seed, is chosen by exactly 16 of the 64 tokens of every device; no expert is chosen by more than 16 of the tokens of one device. `bwd_route`: at every section one expert, drawn from the seed, is chosen by exactly 16 of the 64 tokens of every device; no expert is chosen by more than 16 of the tokens of one device.
All inputs are finite; a program needn't handle non-finite values.
Results may differ from the reference program's by a relative error of at most 0.009.
Values may be sent and summed in bfloat16 or wider, within the bound.
A program may use at most 192 MiB of HBM per device.

```python
import jax
import jax.numpy as jnp
from jax import lax

D = 7168
FF = 1024
EXPERTS = 8
TOK_DEV = 64
TOKENS = 2048
SHARDS = 4
HID_DEV = 256
MOST = 16
N_PIPE = 4


def column_field(noise, column_key, spread):
    columns = jnp.exp(jax.random.uniform(column_key, (1, 1, D), jnp.float32, -spread, spread))
    return (noise * columns).astype(jnp.bfloat16)


def route_table(key):
    hot_key, block_key = jax.random.split(key)
    block_total = TOKENS // TOK_DEV
    hottest = jax.random.randint(hot_key, (N_PIPE,), 0, EXPERTS)
    block_keys = jax.random.split(block_key, N_PIPE * block_total)

    def one_block(single_key, hot_expert):
        pick_key, place_key = jax.random.split(single_key)
        picked = jax.random.permutation(pick_key, (EXPERTS - 1) * MOST)[:TOK_DEV - MOST]
        others = (picked // MOST).astype(jnp.int32)
        others = others + (others >= hot_expert).astype(jnp.int32)
        labels = jnp.concatenate([jnp.full((MOST,), hot_expert, jnp.int32), others])
        placing = jax.random.permutation(place_key, TOK_DEV)
        return labels[placing]
    table = jax.vmap(one_block)(block_keys, jnp.repeat(hottest, block_total))
    return table.reshape(N_PIPE, TOKENS, 1).astype(jnp.int32)


def draw_fwd_src(key, part):
    key = jax.random.fold_in(key, 11)
    noise_key, column_key = jax.random.split(key)
    shape = (N_PIPE, TOKENS, D)
    noise = jnp.clip(jax.random.normal(noise_key, shape, jnp.float32), -4.0, 4.0)
    return column_field(noise, column_key, 1.1513)


def draw_bwd_input(key, part):
    key = jax.random.fold_in(key, 13)
    noise_key, column_key = jax.random.split(key)
    shape = (N_PIPE, TOKENS, D)
    noise = jnp.clip(jax.random.normal(noise_key, shape, jnp.float32), -4.0, 4.0)
    return column_field(noise, column_key, 1.1513)


def draw_fwd_route(key, part):
    key = jax.random.fold_in(key, 21)
    return route_table(key)


def draw_bwd_route(key, part):
    key = jax.random.fold_in(key, 23)
    return route_table(key)


def level_of(stream_key, shape, cuts, smallest, top_value):
    def one(dim, shards_of):
        heights = jax.random.uniform(jax.random.fold_in(jax.random.fold_in(stream_key, 6), dim), (shards_of,), jnp.float32, smallest / len(cuts), top_value / len(cuts))
        return jnp.repeat(jnp.exp(heights), shape[dim] // shards_of).reshape((-1,) + (1,) * (len(shape) - dim - 1))

    level = one(*cuts[0])
    for cut in cuts[1:]:
        level = level * one(*cut)
    return level


def scatter_about(stream_key, shape, width, limit, cuts=(), kind=jnp.bfloat16):
    drawn = width * jax.random.normal(stream_key, shape, jnp.float32)
    if cuts:
        drawn = drawn * level_of(stream_key, shape, cuts, -0.22, 0.18)
    return jnp.clip(drawn, -limit, limit).astype(kind)


def setup_inputs(seed: int = 0) -> dict:
    keys = jax.random.split(jax.random.key(seed), 12)
    return {
        "fwd_src": draw_fwd_src(jax.random.fold_in(keys[11], 71), 0),
        "fwd_route": draw_fwd_route(jax.random.fold_in(keys[11], 71), 0),
        "bwd_input": draw_bwd_input(jax.random.fold_in(keys[11], 71), 0),
        "bwd_expert_out": scatter_about(keys[3], (N_PIPE, TOKENS, D), 0.6, 4.0, ((0, 4), (1, 32))),
        "grad_src": scatter_about(keys[4], (N_PIPE, TOKENS, D), 1.0, 5.0, ((0, 4), (1, 32))),
        "bwd_route": draw_bwd_route(jax.random.fold_in(keys[11], 71), 0),
        "norm_gain": jnp.clip(1.0 + 0.18 * jax.random.normal(keys[6], (N_PIPE, D), jnp.float32), 0.099609375, 1.8984375).astype(jnp.bfloat16),
        "router": scatter_about(keys[7], (N_PIPE, D, EXPERTS), D ** -0.5, 0.0625, ((0, 4),)),
        "gate_w": scatter_about(keys[8], (N_PIPE, D, EXPERTS * FF), D ** -0.5, 0.0625, ((0, 4), (2, 32))),
        "up_w": scatter_about(keys[9], (N_PIPE, D, EXPERTS * FF), D ** -0.5, 0.0625, ((0, 4), (2, 32))),
        "down_w": scatter_about(keys[10], (N_PIPE, EXPERTS * FF, D), FF ** -0.5, 0.1875, ((0, 4), (1, 32))),
    }


norm_eps = 1e-06
route_scale = 2.5

def rms_norm(values, gain_row):
    widened = values.astype(jnp.float32)
    inv_scale = lax.rsqrt(lax.optimization_barrier(jnp.mean(widened * widened, axis=-1, keepdims=True)) + norm_eps)
    normed = (widened * inv_scale * gain_row.astype(jnp.float32)).astype(jnp.bfloat16)
    return (normed, inv_scale)

def expert_weights(gate_section, up_section, down_section, expert_id):
    first_col = (expert_id * FF).astype(jnp.int32)
    return (lax.dynamic_slice_in_dim(gate_section, first_col, FF, 1), lax.dynamic_slice_in_dim(up_section, first_col, FF, 1), lax.dynamic_slice_in_dim(down_section, first_col, FF, 0))

def forward_rows(pieces, gate_part, up_part, down_part):
    rows_in = pieces[0]
    gate_pre = jnp.dot(rows_in, gate_part, preferred_element_type=jnp.float32)
    up_pre = jnp.dot(rows_in, up_part, preferred_element_type=jnp.float32)
    hidden = (jax.nn.silu(gate_pre) * up_pre).astype(jnp.bfloat16)
    total = jnp.zeros((rows_in.shape[0], down_part.shape[1]), jnp.float32)
    for shard_index in range(SHARDS):
        lower_edge = shard_index * HID_DEV
        shard_out = jnp.dot(hidden[:, lower_edge:lower_edge + HID_DEV], down_part[lower_edge:lower_edge + HID_DEV], preferred_element_type=jnp.float32).astype(jnp.bfloat16)
        total = total + lax.optimization_barrier(shard_out).astype(jnp.float32)
    return total

def backward_rows(pieces, gate_part, up_part, down_part):
    rows_in, grads_in = pieces
    gate_pre = jnp.dot(rows_in, gate_part, preferred_element_type=jnp.float32)
    up_pre = jnp.dot(rows_in, up_part, preferred_element_type=jnp.float32)
    gate_sigmoid = jax.nn.sigmoid(gate_pre)
    back_hidden = lax.dot_general(grads_in, down_part, (((1,), (1,)), ((), ())), preferred_element_type=jnp.float32)
    d_gate = (back_hidden * up_pre * gate_sigmoid * (1.0 + gate_pre * (1.0 - gate_sigmoid))).astype(jnp.bfloat16)
    d_up = (back_hidden * gate_pre * gate_sigmoid).astype(jnp.bfloat16)
    total = jnp.zeros((rows_in.shape[0], gate_part.shape[0]), jnp.float32)
    for shard_index in range(SHARDS):
        lower_edge = shard_index * HID_DEV
        upper_edge = lower_edge + HID_DEV
        shard_in = lax.dot_general(d_gate[:, lower_edge:upper_edge], gate_part[:, lower_edge:upper_edge], (((1,), (1,)), ((), ())), preferred_element_type=jnp.float32)
        shard_in = shard_in + lax.dot_general(d_up[:, lower_edge:upper_edge], up_part[:, lower_edge:upper_edge], (((1,), (1,)), ((), ())), preferred_element_type=jnp.float32)
        shard_in = shard_in.astype(jnp.bfloat16)
        total = total + lax.optimization_barrier(shard_in).astype(jnp.float32)
    return total

def expert_rows(pieces, chosen, compute, gate_section, up_section, down_section):
    row_count = chosen.shape[0]
    block_rows = TOK_DEV
    block_count = row_count // block_rows + EXPERTS
    order = jnp.argsort(chosen, stable=True).astype(jnp.int32)
    sorted_ids = chosen[order]
    one_hot = (chosen[:, None] == jnp.arange(EXPERTS, dtype=jnp.int32)[None, :]).astype(jnp.int32)
    counts = lax.optimization_barrier(jnp.sum(one_hot, axis=0)).astype(jnp.int32)
    padded = ((counts + block_rows - 1) // block_rows * block_rows).astype(jnp.int32)
    starts = (jnp.cumsum(padded) - padded).astype(jnp.int32)
    firsts = (jnp.cumsum(counts) - counts).astype(jnp.int32)
    in_group = jnp.arange(row_count, dtype=jnp.int32) - firsts[sorted_ids]
    target = (starts[sorted_ids] + in_group).astype(jnp.int32)
    ends = starts + padded
    block_start = jnp.arange(block_count, dtype=jnp.int32) * block_rows
    owner = jnp.minimum(lax.optimization_barrier(jnp.sum((block_start[:, None] >= ends[None, :]).astype(jnp.int32), axis=1)), EXPERTS - 1)
    owner = owner.astype(jnp.int32)
    stacked = tuple((jnp.zeros((block_count * block_rows, piece.shape[1]), piece.dtype).at[target].set(piece[order]).reshape(block_count, block_rows, piece.shape[1]) for piece in pieces))

    def one_block(item):
        block_pieces, expert_id = item
        gate_part, up_part, down_part = expert_weights(gate_section, up_section, down_section, expert_id)
        return compute(block_pieces, gate_part, up_part, down_part)
    results = lax.map(one_block, (stacked, owner))
    results = results.reshape(block_count * block_rows, results.shape[2])
    return jnp.zeros((row_count, results.shape[1]), jnp.float32).at[order].set(results[target])

def route_weight(normed, router_section, one_hot):
    logits = jnp.dot(normed, router_section, preferred_element_type=jnp.float32)
    return jax.nn.sigmoid(lax.optimization_barrier(jnp.sum(logits * one_hot, axis=1)))

def section_forward(arriving, gain_row, router_section, route_section, gate_section, up_section, down_section):
    normed, inv_scale = rms_norm(arriving, gain_row)
    chosen = route_section[:, 0].astype(jnp.int32)
    one_hot = (chosen[:, None] == jnp.arange(EXPERTS, dtype=jnp.int32)[None, :]).astype(jnp.float32)
    weight = route_weight(normed, router_section, one_hot)
    expert_sum = expert_rows((normed,), chosen, forward_rows, gate_section, up_section, down_section)
    return (arriving.astype(jnp.float32) + route_scale * weight[:, None] * expert_sum).astype(jnp.bfloat16)

def section_backward(saved_input, incoming, saved_out, gain_row, router_section, route_section, gate_section, up_section, down_section):
    normed, inv_scale = rms_norm(saved_input, gain_row)
    chosen = route_section[:, 0].astype(jnp.int32)
    one_hot = (chosen[:, None] == jnp.arange(EXPERTS, dtype=jnp.int32)[None, :]).astype(jnp.float32)
    weight = route_weight(normed, router_section, one_hot)
    input_sum = expert_rows((normed, incoming), chosen, backward_rows, gate_section, up_section, down_section)
    agreement = lax.optimization_barrier(jnp.sum(incoming.astype(jnp.float32) * saved_out.astype(jnp.float32), axis=1))
    d_logit = route_scale * agreement * weight * (1.0 - weight)
    router_column = lax.dot_general(one_hot.astype(jnp.bfloat16), router_section, (((1,), (1,)), ((), ())), preferred_element_type=jnp.float32)
    d_normed = route_scale * weight[:, None] * input_sum + d_logit[:, None] * router_column
    widened = saved_input.astype(jnp.float32)
    scaled_grad = d_normed * gain_row.astype(jnp.float32)
    d_input = inv_scale * scaled_grad - widened * inv_scale ** 3 * lax.optimization_barrier(jnp.mean(widened * scaled_grad, axis=1, keepdims=True))
    return (incoming.astype(jnp.float32) + d_input).astype(jnp.bfloat16)

def reference(fwd_src, fwd_route, bwd_input, bwd_expert_out, grad_src, bwd_route, norm_gain, router, gate_w, up_w, down_w):
    forward_all = []
    backward_all = []
    for section_index in range(N_PIPE):
        arriving = fwd_src[(section_index - 1) % N_PIPE]
        incoming = grad_src[(section_index + 1) % N_PIPE]
        forward_all.append(section_forward(arriving, norm_gain[section_index], router[section_index], fwd_route[section_index], gate_w[section_index], up_w[section_index], down_w[section_index]))
        backward_all.append(section_backward(bwd_input[section_index], incoming, bwd_expert_out[section_index], norm_gain[section_index], router[section_index], bwd_route[section_index], gate_w[section_index], up_w[section_index], down_w[section_index]))
    return (jnp.stack(forward_all), jnp.stack(backward_all))
```

```python
import functools

import jax
import jax.numpy as jnp
from jax import lax
from jax.experimental import pallas as pl
from jax.experimental.pallas import tpu as pltpu
from jax.sharding import PartitionSpec as P

MESH = pl.DeviceIdType.MESH
BF = jnp.bfloat16
F32 = jnp.float32

D = 7168
Q = 1792
T = 64
E = 8
S = 16
H = 256
ROWS = E * T
SCALE = 2.5
EPS = 1e-06
NT = (((1,), (1,)), ((), ()))
TN = (((0,), (0,)), ((), ()))

OFFS = ((1, 0), (3, 0), (0, 1), (2, 0), (1, 1), (3, 1), (2, 1))


def dot(a, b, dims=(((1,), (0,)), ((), ()))):
    return lax.dot_general(a, b, dims, preferred_element_type=F32)


def kernel(
    fwd_src, fwd_route, bwd_input, bwd_expert_out, grad_src, bwd_route, gain, router_t, gate_w, up_w, down_w,
    fwd_out, bwd_out,
    bi, arr, inc, beo, nb, nf, xb, xf, xi, sbh, sbi, rbb, rbi, rbf, rrb, rrf, fb, ff,
    wown, wn, wd, ptb, ptf, acc, ps, pr, bacc, bs, br, dgu, dgn, hid, sg, col,
    ld, pipe_s, pipe_r, pt_s, pt_r, w_s, w_r, wd_s, wd_r, xb_s, xb_r, xf_s, xf_r, xi_s, xi_r,
    yb_s, yb_r, yi_s, yi_r, yf_s, yf_r, rs_s, rs_r, bk_s, bk_r, dg_s, dg_r, hd_s, hd_r,
    qb_s, qb_r, qf_s, qf_r, fb_s, fb_r, ff_s, ff_r, out_s,
):
    p = lax.axis_index("pipe")
    ei = lax.axis_index("expert")
    me_e = ei // 4
    y, z, x = ei // 8, me_e % 2, ei % 4
    odd = x % 2

    def at_x(k):
        return (p, me_e * 4 + (x + k) % 4)

    def at_yz(k, l):
        return (p, ((y + k) % 4) * 8 + ((z + l) % 2) * 4 + x)

    def expert_at(k, l):
        return ((y + k) % 4) * 2 + (z + l) % 2

    def at_pipe(k):
        return ((p + k) % 4, ei)

    def qa(xx):
        return xx % 2

    def qb(xx):
        return 3 - xx % 2

    off_a = 1 + 2 * odd
    off_b = 3 - 2 * odd

    sends = []

    def put(src, dst, s_sem, r_sem, device):
        c = pltpu.make_async_remote_copy(
            src_ref=src, dst_ref=dst, send_sem=s_sem, recv_sem=r_sem, device_id=device, device_id_type=MESH
        )
        c.start()
        return c

    def post(*args):
        sends.append(put(*args))

    def got(ref, sem):
        pltpu.make_async_copy(ref, ref, sem).wait()

    def local(src, dst, sem):
        c = pltpu.make_async_copy(src, dst, sem)
        c.start()
        return c

    def cols(q):
        return pl.ds(pl.multiple_of(q * Q, 128), Q)

    load_bi = [local(bwd_input.at[:, pl.ds(q * Q, Q)], bi.at[q], ld.at[q]) for q in range(4)]

    barrier = pltpu.get_barrier_semaphore()
    peers = [at_x(k) for k in (1, 2, 3)] + [at_yz(k, l) for k, l in OFFS] + [at_pipe(1), at_pipe(3)]
    for peer in peers:
        pl.semaphore_signal(barrier, inc=1, device_id=peer, device_id_type=MESH)
    pl.semaphore_wait(barrier, len(peers))

    for q in range(4):
        post(grad_src.at[:, pl.ds(q * Q, Q)], inc.at[q], pipe_s.at[0, q], pipe_r.at[0, q], at_pipe(3))
    for q in range(4):
        post(fwd_src.at[:, pl.ds(q * Q, Q)], arr.at[q], pipe_s.at[1, q], pipe_r.at[1, q], at_pipe(1))

    def slots(route, table):
        chosen = route[...].astype(F32)
        lane = lax.broadcasted_iota(jnp.int32, (T, E * S), 1).astype(F32)
        hot = (lane == chosen).astype(F32)
        low = (
            lax.broadcasted_iota(jnp.int32, (T, T), 0) > lax.broadcasted_iota(jnp.int32, (T, T), 1)
        ).astype(F32)
        prior = dot(low.astype(BF), hot.astype(BF))
        rank = jnp.sum(prior * hot, axis=1, keepdims=True)
        table[0] = (lane == chosen * S + rank).astype(F32).astype(BF)

    slots(bwd_route, ptb)
    slots(fwd_route, ptf)
    for i, table in enumerate((ptb, ptf)):
        for k in (1, 2, 3):
            post(table.at[0], table.at[4 - k], pt_s.at[i, k], pt_r.at[i, 4 - k], at_x(k))

    def rms_norm(v, normed, keep):
        def rows(i, _):
            r = pl.ds(pl.multiple_of(i * 16, 16), 16)
            total = jnp.zeros((16, 1), F32)
            for q in range(4):
                w = v[q, r, :].astype(F32)
                total += jnp.sum(w * w, axis=1, keepdims=True)
            inv = lax.rsqrt(total * (1.0 / D) + EPS)
            if keep is not None:
                col[keep, r, :] = jnp.broadcast_to(inv, (16, 128))
            for q in range(4):
                normed[q, r, :] = (v[q, r, :].astype(F32) * inv * gain[q]).astype(BF)
            return 0

        lax.fori_loop(0, 4, rows, 0)

    def route_weight(normed, route, keep):
        logits = jnp.zeros((T, E), F32)
        for q in range(4):
            logits += dot(normed[q], router_t[q].astype(BF), NT)
        hot = (lax.broadcasted_iota(jnp.int32, (T, E), 1) == route[...]).astype(F32)
        weight = jax.nn.sigmoid(jnp.sum(logits * hot, axis=1, keepdims=True))
        col[keep] = jnp.broadcast_to(weight, (T, 128))

    def spread_half(normed, xs, s_sem, r_sem):
        out = []
        for j, quarter in enumerate((qa, qb)):
            local(normed.at[quarter(x)], xs.at[0, j], r_sem.at[0, j])
            for k in (1, 3, 2):
                out.append(
                    put(normed.at[quarter(x + k)], xs.at[4 - k, j], s_sem.at[k, j], r_sem.at[4 - k, j], at_x(k))
                )
        return out

    for c in load_bi:
        c.wait()
    rms_norm(bi, nb, 0)
    nb_sends = spread_half(nb, xb, xb_s, xb_r)

    for i, w in enumerate((gate_w, up_w)):
        post(w.at[qa(x + 1)], wn.at[0, i], w_s.at[0, i], w_r.at[0, i], at_x(off_a))
        post(w.at[qb(x + 1)], wn.at[1, i], w_s.at[1, i], w_r.at[1, i], at_x(off_b))
        local(w.at[qa(x)], wown.at[i, 0], ld.at[4 + 2 * i])
        local(w.at[qb(x)], wown.at[i, 1], ld.at[5 + 2 * i])

    route_weight(nb, bwd_route, 1)

    for k in (1, 2, 3):
        got(ptb.at[4 - k], pt_r.at[0, 4 - k])
        got(ptf.at[4 - k], pt_r.at[1, 4 - k])

    def place(block, table, dst):
        def one(d, _):
            r = dot(table[d], block(d)[...], TN).astype(BF).reshape(E, S, Q)
            dst[:, pl.ds(pl.multiple_of((x + d) % 4 * S, S), S), :] = r
            return 0

        return one

    def to_experts(src, dst, s_sem, r_sem):
        local(src.at[me_e], dst.at[0], r_sem(0))
        out = []
        for k, l in OFFS:
            back = ((4 - k) % 4) * 2 + l
            out.append(put(src.at[expert_at(k, l)], dst.at[back], s_sem(k * 2 + l), r_sem(back), at_yz(k, l)))
        return out

    def dispatch_half(xs, table, sb, rb, xr, ys, yr):
        out = []
        for j in range(2):
            fill = place(lambda d: xs.at[d, j], table, sb.at[j])

            def one(d, _):
                got(xs.at[d, j], xr.at[d, j])
                return fill(d, 0)

            lax.fori_loop(0, 4, one, 0)
            out += to_experts(sb.at[j], rb.at[j], lambda o: ys.at[o, j], lambda o: yr.at[o, j])
        return out

    yb_sends = dispatch_half(xb, ptb, sbh, rbb, xb_r, yb_s, yb_r)

    for q in range(4):
        got(inc.at[q], pipe_r.at[0, q])
    local(inc.at[x], xi.at[0], xi_r.at[0])
    for k in (1, 3, 2):
        post(inc.at[(x + k) % 4], xi.at[4 - k], xi_s.at[k], xi_r.at[4 - k], at_x(k))

    for q in range(4):
        got(arr.at[q], pipe_r.at[1, q])
    rms_norm(arr, nf, None)
    nf_sends = spread_half(nf, xf, xf_s, xf_r)

    local(down_w.at[:, cols(x)], wd.at[0], ld.at[8])
    for k in (1, 3, 2):
        post(down_w.at[:, cols((x + k) % 4)], wd.at[4 - k], wd_s.at[k], wd_r.at[4 - k], at_x(k))

    load_beo = [local(bwd_expert_out.at[:, pl.ds(q * Q, Q)], beo.at[q], ld.at[9 + q]) for q in range(4)]

    fill_i = place(lambda d: xi.at[d], ptb, sbi)

    def one_i(d, _):
        got(xi.at[d], xi_r.at[d])
        return fill_i(d, 0)

    lax.fori_loop(0, 4, one_i, 0)
    sends += to_experts(sbi, rbi, lambda o: yi_s.at[o], lambda o: yi_r.at[o])

    route_weight(nf, fwd_route, 2)

    for j in range(2):
        got(rbb.at[j, 0], yb_r.at[0, j])
    for c in yb_sends:
        c.wait_send()
    sends += dispatch_half(xf, ptf, sbh, rbf, xf_r, yf_s, yf_r)

    for c in load_beo:
        c.wait()

    def agree(i, _):
        r = pl.ds(pl.multiple_of(i * 16, 16), 16)
        total = jnp.zeros((16, 1), F32)
        for q in range(4):
            total += jnp.sum(inc[q, r, :].astype(F32) * beo[q, r, :].astype(F32), axis=1, keepdims=True)
        col[3, r, :] = jnp.broadcast_to(total, (16, 128))
        return 0

    lax.fori_loop(0, 4, agree, 0)

    def gate_up(rb, i):
        def one(n, _):
            w, m = n // 2, n % 2
            r = pl.ds(pl.multiple_of(m * 256, 256), 256)
            m4 = pl.ds(m * 4, 4)
            ra = rb[0, m4].reshape(256, Q)
            acc[w, r, :] = dot(ra, wown[w, 0])
            ps[i, 0, w, r, :] = dot(ra, wn[0, w]).astype(BF)
            rc = rb[1, m4].reshape(256, Q)
            acc[w, r, :] += dot(rc, wown[w, 1])
            ps[i, 1, w, r, :] = dot(rc, wn[1, w]).astype(BF)
            return 0

        lax.fori_loop(0, 4, one, 0)
        post(ps.at[i, 0], pr.at[i, 0], rs_s.at[i, 0], rs_r.at[i, 0], at_x(off_a))
        post(ps.at[i, 1], pr.at[i, 1], rs_s.at[i, 1], rs_r.at[i, 1], at_x(off_b))

    for i in range(2):
        for j in range(2):
            got(wn.at[j, i], w_r.at[j, i])
            got(wown.at[i, j], ld.at[4 + 2 * i + j])
    for j in range(2):
        for o in range(1, 8):
            got(rbb.at[j, o], yb_r.at[o, j])
    gate_up(rbb, 0)

    got(wd.at[0], ld.at[8])
    for d in (1, 2, 3):
        got(wd.at[d], wd_r.at[d])
    for o in range(8):
        got(rbi.at[o], yi_r.at[o])

    def back_own(m, _):
        r = pl.ds(pl.multiple_of(m * 256, 256), 256)
        bacc[r, :] = dot(rbi[pl.ds(m * 4, 4)].reshape(256, Q), wd[0], NT)
        return 0

    def back_other(n, _):
        d, m = 1 + n // 2, n % 2
        r = pl.ds(pl.multiple_of(m * 256, 256), 256)
        bs[d, r, :] = dot(rbi[pl.ds(m * 4, 4)].reshape(256, Q), wd[d], NT).astype(BF)
        return 0

    lax.fori_loop(0, 6, back_other, 0)
    for k in (1, 3, 2):
        post(bs.at[k], br.at[4 - k], bk_s.at[k], bk_r.at[4 - k], at_x(k))
    lax.fori_loop(0, 2, back_own, 0)

    for j in range(2):
        got(pr.at[0, j], rs_r.at[0, j])
    for d in (1, 2, 3):
        got(br.at[d], bk_r.at[d])

    def act_b(m, _):
        r = pl.ds(pl.multiple_of(m * 32, 32), 32)
        g = acc[0, r, :] + pr[0, 0, 0, r, :].astype(F32) + pr[0, 1, 0, r, :].astype(F32)
        u = acc[1, r, :] + pr[0, 0, 1, r, :].astype(F32) + pr[0, 1, 1, r, :].astype(F32)
        b = bacc[r, :] + br[1, r, :].astype(F32) + br[2, r, :].astype(F32) + br[3, r, :].astype(F32)
        s = jax.nn.sigmoid(g)
        dgu[0, r, :] = (b * u * s * (1.0 + g * (1.0 - s))).astype(BF)
        dgu[1, r, :] = (b * g * s).astype(BF)
        return 0

    lax.fori_loop(0, ROWS // 32, act_b, 0)
    post(dgu, dgn.at[0], dg_s.at[0], dg_r.at[0], at_x(off_a))
    post(dgu, dgn.at[1], dg_s.at[1], dg_r.at[1], at_x(off_b))

    for j in range(2):
        for o in range(8):
            got(rbf.at[j, o], yf_r.at[o, j])
    gate_up(rbf, 1)

    def back_home(src, dst, s_sem, r_sem):
        local(src.at[0], dst.at[me_e], r_sem(0))
        for k, l in OFFS:
            back = ((4 - k) % 4) * 2 + l
            post(src.at[k * 2 + l], dst.at[me_e], s_sem(k * 2 + l), r_sem(back), at_yz(k, l))

    for j in range(2):
        got(dgn.at[j], dg_r.at[j])

        def cols_b(n, _):
            c = pl.ds(pl.multiple_of(n * 256, 256), 256)
            r = dot(dgu[0], wown[0, j, c, :], NT)
            r += dot(dgu[1], wown[1, j, c, :], NT)
            r += dot(dgn[j, 0], wn[j, 0, c, :], NT)
            r += dot(dgn[j, 1], wn[j, 1, c, :], NT)
            rbb[j, :, :, c] = r.astype(BF).reshape(E, T, 256)
            return 0

        lax.fori_loop(0, Q // 256, cols_b, 0)
        back_home(rbb.at[j], rrb.at[j], lambda o: qb_s.at[o, j], lambda o: qb_r.at[o, j])

    for j in range(2):
        got(pr.at[1, j], rs_r.at[1, j])

    def act_f(m, _):
        r = pl.ds(pl.multiple_of(m * 32, 32), 32)
        g = acc[0, r, :] + pr[1, 0, 0, r, :].astype(F32) + pr[1, 1, 0, r, :].astype(F32)
        u = acc[1, r, :] + pr[1, 0, 1, r, :].astype(F32) + pr[1, 1, 1, r, :].astype(F32)
        hid[0, r, :] = (g * jax.nn.sigmoid(g) * u).astype(BF)
        return 0

    lax.fori_loop(0, ROWS // 32, act_f, 0)
    for k in (1, 3, 2):
        post(hid.at[0], hid.at[4 - k], hd_s.at[k], hd_r.at[4 - k], at_x(k))
    for d in (1, 2, 3):
        got(hid.at[d], hd_r.at[d])

    def cols_f(n, _):
        c = pl.ds(pl.multiple_of(n * 256, 256), 256)
        r = dot(hid[0], wd[0, :, c])
        for d in (1, 2, 3):
            r += dot(hid[d], wd[d, :, c])
        rbi[:, :, c] = r.astype(BF).reshape(E, T, 256)
        return 0

    lax.fori_loop(0, Q // 256, cols_f, 0)
    back_home(rbi, rrf, lambda o: qf_s.at[o], lambda o: qf_r.at[o])

    def unplace(src, table, dst):
        def one(d, _):
            rows = src[:, pl.ds(pl.multiple_of((x + d) % 4 * S, S), S), :].reshape(E * S, Q)
            dst(d)[...] = dot(table[d], rows).astype(BF)
            return 0

        lax.fori_loop(0, 4, one, 0)

    for j in range(2):
        for o in range(8):
            got(rrb.at[j, 0], qb_r.at[o, j])
        unplace(rrb.at[j], ptb, lambda d: xb.at[d, j])
        for k in (1, 3, 2):
            post(xb.at[k, j], fb.at[4 - k, j], fb_s.at[k, j], fb_r.at[4 - k, j], at_x(k))

    for o in range(8):
        got(rrf.at[0], qf_r.at[o])
    unplace(rrf, ptf, lambda d: xi.at[d])
    for k in (1, 3, 2):
        post(xi.at[k], ff.at[4 - k], ff_s.at[k], ff_r.at[4 - k], at_x(k))

    for c in nb_sends + nf_sends:
        c.wait_send()
    for j in range(2):
        for d in (1, 2, 3):
            got(fb.at[d, j], fb_r.at[d, j])
    quarters = ((qa(x), 0, 0), (qb(x), 0, 1), (qa(x + 1), 1, 0), (qb(x + 1), 1, 1))

    def finish_b(i, _):
        r = pl.ds(pl.multiple_of(i * 16, 16), 16)
        inv = col[0, r, 0:1]
        weight = col[1, r, 0:1]
        d_logit = SCALE * col[3, r, 0:1] * weight * (1.0 - weight)
        hot = (lax.broadcasted_iota(jnp.int32, (16, E), 1) == bwd_route[r, :]).astype(BF)
        total = jnp.zeros((16, 1), F32)
        for q, other, j in quarters:
            if other:
                g = fb[1, j, r, :].astype(F32) + fb[3, j, r, :].astype(F32)
            else:
                g = xb[0, j, r, :].astype(F32) + fb[2, j, r, :].astype(F32)
            dn = SCALE * weight * g + d_logit * dot(hot, router_t[q].astype(BF))
            s = dn * gain[q]
            sg[q, r, :] = s
            total += jnp.sum(s * bi[q, r, :].astype(F32), axis=1, keepdims=True)
        factor = inv * inv * inv * (total * (1.0 / D))
        for q in range(4):
            v = bi[q, r, :].astype(F32)
            o = inc[q, r, :].astype(F32) + (inv * sg[q, r, :] - v * factor)
            nb[q, r, :] = o.astype(BF)
        return 0

    lax.fori_loop(0, 4, finish_b, 0)
    outs = [local(nb.at[q], bwd_out.at[:, pl.ds(q * Q, Q)], out_s.at[0, q]) for q in range(4)]

    for d in (1, 2, 3):
        got(ff.at[d], ff_r.at[d])

    def finish_f(i, _):
        r = pl.ds(pl.multiple_of(i * 16, 16), 16)
        weight = col[2, r, 0:1]
        for d in range(4):
            q = (x + d) % 4
            e = (xi[0, r, :] if d == 0 else ff[d, r, :]).astype(F32)
            nf[q, r, :] = (arr[q, r, :].astype(F32) + SCALE * weight * e).astype(BF)
        return 0

    lax.fori_loop(0, 4, finish_f, 0)
    outs += [local(nf.at[q], fwd_out.at[:, pl.ds(q * Q, Q)], out_s.at[1, q]) for q in range(4)]

    for c in sends:
        c.wait_send()
    for c in outs:
        c.wait()


def shards(
    fwd_src, fwd_route, bwd_input, bwd_expert_out, grad_src, bwd_route, norm_gain, router, gate_w, up_w, down_w
):
    gain = norm_gain[0].astype(F32).reshape(4, 1, Q)
    router_t = router[0].T.astype(F32).reshape(E, 4, Q).transpose(1, 0, 2)
    hbm = pl.BlockSpec(memory_space=pl.ANY)
    vmem = pl.BlockSpec(memory_space=pltpu.VMEM)
    dma = pltpu.SemaphoreType.DMA

    def buf(*shape, dtype=BF):
        return pltpu.VMEM(shape, dtype)

    scratch = [
        buf(4, T, Q), buf(4, T, Q), buf(4, T, Q), buf(4, T, Q),
        buf(4, T, Q), buf(4, T, Q),
        buf(4, 2, T, Q), buf(4, 2, T, Q), buf(4, T, Q),
        buf(2, E, T, Q), buf(E, T, Q),
        buf(2, E, T, Q), buf(E, T, Q), buf(2, E, T, Q),
        buf(2, E, T, Q), buf(E, T, Q),
        buf(4, 2, T, Q), buf(4, T, Q),
        buf(2, 2, Q, H), buf(2, 2, Q, H), buf(4, H, Q),
        buf(4, T, E * S), buf(4, T, E * S),
        buf(2, ROWS, H, dtype=F32), buf(2, 2, 2, ROWS, H), buf(2, 2, 2, ROWS, H),
        buf(ROWS, H, dtype=F32), buf(4, ROWS, H), buf(4, ROWS, H),
        buf(2, ROWS, H), buf(2, 2, ROWS, H), buf(4, ROWS, H),
        buf(4, T, Q, dtype=F32), buf(4, T, 128, dtype=F32),
        dma((16,)), dma((2, 4)), dma((2, 4)), dma((2, 4)), dma((2, 4)),
        dma((2, 2)), dma((2, 2)), dma((4,)), dma((4,)),
        dma((4, 2)), dma((4, 2)), dma((4, 2)), dma((4, 2)), dma((4,)), dma((4,)),
        dma((8, 2)), dma((8, 2)), dma((8,)), dma((8,)), dma((8, 2)), dma((8, 2)),
        dma((2, 2)), dma((2, 2)), dma((4,)), dma((4,)), dma((2,)), dma((2,)), dma((4,)), dma((4,)),
        dma((8, 2)), dma((8, 2)), dma((8,)), dma((8,)),
        dma((4, 2)), dma((4, 2)), dma((4,)), dma((4,)), dma((2, 4)),
    ]
    out = jax.ShapeDtypeStruct((T, D), BF)
    fwd_out, bwd_out = pl.pallas_call(
        kernel,
        out_shape=(out, out),
        in_specs=[hbm, vmem, hbm, hbm, hbm, vmem, vmem, vmem, hbm, hbm, hbm],
        out_specs=(hbm, hbm),
        scratch_shapes=scratch,
        compiler_params=pltpu.CompilerParams(
            collective_id=0, has_side_effects=True, vmem_limit_bytes=62 * 1024 * 1024
        ),
        cost_estimate=pl.CostEstimate(
            flops=15_000_000_000, bytes_accessed=20_000_000, transcendentals=400_000
        ),
    )(
        fwd_src[0],
        fwd_route[0],
        bwd_input[0],
        bwd_expert_out[0],
        grad_src[0],
        bwd_route[0],
        gain,
        router_t,
        gate_w[0].reshape(4, Q, H),
        up_w[0].reshape(4, Q, H),
        down_w[0],
    )
    return (fwd_out[None], bwd_out[None])


def solution(mesh):
    placed = (
        P("pipe", "expert", None),
        P("pipe", "expert", None),
        P("pipe", "expert", None),
        P("pipe", "expert", None),
        P("pipe", "expert", None),
        P("pipe", "expert", None),
        P("pipe", None),
        P("pipe", None, None),
        P("pipe", None, "expert"),
        P("pipe", None, "expert"),
        P("pipe", "expert", None),
    )
    return jax.shard_map(
        shards,
        mesh=mesh,
        in_specs=placed,
        out_specs=(P("pipe", "expert", None), P("pipe", "expert", None)),
        check_vma=False,
    )
```

```python
import functools

import jax
import jax.numpy as jnp
from jax import lax
from jax.experimental import pallas as pl
from jax.experimental.pallas import tpu as pltpu
from jax.sharding import PartitionSpec as P

MESH = pl.DeviceIdType.MESH
BF = jnp.bfloat16
F32 = jnp.float32

D = 7168
Q = 1792
T = 64
E = 8
S = 16
H = 256
ROWS = E * T
SCALE = 2.5
EPS = 1e-06
NT = (((1,), (1,)), ((), ()))
TN = (((0,), (0,)), ((), ()))

OFFS = ((1, 0), (3, 0), (0, 1), (2, 0), (1, 1), (3, 1), (2, 1))


def dot(a, b, dims=(((1,), (0,)), ((), ()))):
    return lax.dot_general(a, b, dims, preferred_element_type=F32)


def kernel(
    fwd_src, fwd_route, bwd_input, bwd_expert_out, grad_src, bwd_route, gain_row, router_t, gate_w, up_w, down_w,
    fwd_out, bwd_out,
    bi, arr, inc, beo, nb, nf, xb, xf, xi, sbh, sbi, rbb, rbi, rbf, rrb, rrf, rrc, gb, gs, fb, ff,
    wown, wn, wd, ptb, ptf, acc, ps, pr, bacc, bs, br, dgu, dgn, hid, sg, col, gain,
    ld, pipe_s, pipe_r, pt_s, pt_r, w_s, w_r, wd_s, wd_r, xb_s, xb_r, xf_s, xf_r, xi_s, xi_r,
    yb_s, yb_r, yi_s, yi_r, yf_s, yf_r, rs_s, rs_r, bk_s, bk_r, dg_s, dg_r, hd_s, hd_r,
    gb_s, gb_r, qb_s, qb_r, qc_s, qc_r, qf_s, qf_r, fb_s, fb_r, ff_s, ff_r, out_s,
):
    p = lax.axis_index("pipe")
    ei = lax.axis_index("expert")
    me_e = ei // 4
    y, z, x = ei // 8, me_e % 2, ei % 4
    odd = x % 2

    def at_x(k):
        return (p, me_e * 4 + (x + k) % 4)

    def at_yz(k, l):
        return (p, ((y + k) % 4) * 8 + ((z + l) % 2) * 4 + x)

    def expert_at(k, l):
        return ((y + k) % 4) * 2 + (z + l) % 2

    def at_pipe(k):
        return ((p + k) % 4, ei)

    def qa(xx):
        return xx % 2

    def qb(xx):
        return 3 - xx % 2

    off_a = 1 + 2 * odd
    off_b = 3 - 2 * odd

    sends = []

    def put(src, dst, s_sem, r_sem, device):
        c = pltpu.make_async_remote_copy(
            src_ref=src, dst_ref=dst, send_sem=s_sem, recv_sem=r_sem, device_id=device, device_id_type=MESH
        )
        c.start()
        return c

    def post(*args):
        sends.append(put(*args))

    def got(ref, sem):
        pltpu.make_async_copy(ref, ref, sem).wait()

    def local(src, dst, sem):
        c = pltpu.make_async_copy(src, dst, sem)
        c.start()
        return c

    def cols(q):
        return pl.ds(pl.multiple_of(q * Q, 128), Q)

    load_bi = [local(bwd_input.at[:, pl.ds(q * Q, Q)], bi.at[q], ld.at[q]) for q in range(4)]

    barrier = pltpu.get_barrier_semaphore()
    peers = [at_x(k) for k in (1, 2, 3)] + [at_yz(k, l) for k, l in OFFS] + [at_pipe(1), at_pipe(3)]
    for peer in peers:
        pl.semaphore_signal(barrier, inc=1, device_id=peer, device_id_type=MESH)
    pl.semaphore_wait(barrier, len(peers))

    def swap_weights(i, w):
        post(w.at[qa(x + 1)], wn.at[0, i], w_s.at[0, i], w_r.at[0, i], at_x(off_a))
        post(w.at[qb(x + 1)], wn.at[1, i], w_s.at[1, i], w_r.at[1, i], at_x(off_b))

    def slots(route, table, keep):
        row = lax.broadcasted_iota(jnp.int32, (T, T), 0)
        lower = lax.broadcasted_iota(jnp.int32, (T, T), 1)
        eye = (row == lower).astype(F32)
        chosen = jnp.sum(eye * route[...].astype(F32), axis=1, keepdims=True)
        col[keep] = jnp.broadcast_to(chosen, (T, 128))
        lane = lax.broadcasted_iota(jnp.int32, (T, E * S), 1).astype(F32)
        hot = (lane == chosen).astype(F32)
        low = (row > lower).astype(F32)
        prior = dot(low.astype(BF), hot.astype(BF))
        rank = jnp.sum(prior * hot, axis=1, keepdims=True)
        table[0] = (lane == chosen * S + rank).astype(F32).astype(BF)

    slots(bwd_route, ptb, 4)
    slots(fwd_route, ptf, 5)
    for i, table in enumerate((ptb, ptf)):
        for k in (1, 2, 3):
            post(table.at[0], table.at[4 - k], pt_s.at[i, k], pt_r.at[i, 4 - k], at_x(k))

    def rms_norm(v, normed, keep):
        def rows(i, _):
            r = pl.ds(pl.multiple_of(i * 16, 16), 16)
            total = jnp.zeros((16, 1), F32)
            for q in range(4):
                w = v[q, r, :].astype(F32)
                total += jnp.sum(w * w, axis=1, keepdims=True)
            inv = lax.rsqrt(total * (1.0 / D) + EPS)
            if keep is not None:
                col[keep, r, :] = jnp.broadcast_to(inv, (16, 128))
            for q in range(4):
                normed[q, r, :] = (v[q, r, :].astype(F32) * inv * gain[q]).astype(BF)
            return 0

        lax.fori_loop(0, 4, rows, 0)

    def route_weight(normed, chosen, keep):
        logits = jnp.zeros((T, E), F32)
        for q in range(4):
            logits += dot(normed[q], router_t[:, q * Q : (q + 1) * Q], NT)
        hot = (lax.broadcasted_iota(jnp.int32, (T, E), 1).astype(F32) == col[chosen, :, 0:1]).astype(F32)
        weight = jax.nn.sigmoid(jnp.sum(logits * hot, axis=1, keepdims=True))
        col[keep] = jnp.broadcast_to(weight, (T, 128))

    def spread_half(j, normed, xs, s_sem, r_sem):
        quarter = (qa, qb)[j]
        local(normed.at[quarter(x)], xs.at[0, j], r_sem.at[0, j])
        return [
            put(normed.at[quarter(x + k)], xs.at[4 - k, j], s_sem.at[k, j], r_sem.at[4 - k, j], at_x(k))
            for k in (1, 3, 2)
        ]

    def place(block, table, dst):
        def one(d, _):
            r = dot(table[d], block(d)[...], TN).astype(BF).reshape(E, S, Q)
            dst[:, pl.ds(pl.multiple_of((x + d) % 4 * S, S), S), :] = r
            return 0

        return one

    def to_experts(src, dst, s_sem, r_sem):
        local(src.at[me_e], dst.at[0], r_sem(0))
        out = []
        for k, l in OFFS:
            back = ((4 - k) % 4) * 2 + l
            out.append(put(src.at[expert_at(k, l)], dst.at[back], s_sem(k * 2 + l), r_sem(back), at_yz(k, l)))
        return out

    def dispatch_half(j, xs, table, sb, rb, xr, ys, yr):
        fill = place(lambda d: xs.at[d, j], table, sb.at[j])

        def one(d, _):
            got(xs.at[d, j], xr.at[d, j])
            return fill(d, 0)

        lax.fori_loop(0, 4, one, 0)
        return to_experts(sb.at[j], rb.at[j], lambda o: ys.at[o, j], lambda o: yr.at[o, j])

    def gate_up(rb, i):
        def one(n, _):
            w, m = n // 2, n % 2
            r = pl.ds(pl.multiple_of(m * 256, 256), 256)
            m4 = pl.ds(m * 4, 4)
            ra = rb[0, m4].reshape(256, Q)
            acc[i, w, r, :] = dot(ra, wown[w, 0])
            ps[i, 0, w, r, :] = dot(ra, wn[0, w]).astype(BF)
            rc = rb[1, m4].reshape(256, Q)
            acc[i, w, r, :] += dot(rc, wown[w, 1])
            ps[i, 1, w, r, :] = dot(rc, wn[1, w]).astype(BF)
            return 0

        lax.fori_loop(0, 4, one, 0)

    def swap_parts(i):
        post(ps.at[i, 0], pr.at[i, 0], rs_s.at[i, 0], rs_r.at[i, 0], at_x(off_a))
        post(ps.at[i, 1], pr.at[i, 1], rs_s.at[i, 1], rs_r.at[i, 1], at_x(off_b))

    def back_home(src, dst, s_sem, r_sem):
        local(src.at[0], dst.at[me_e], r_sem(0))
        for k, l in OFFS:
            back = ((4 - k) % 4) * 2 + l
            post(src.at[k * 2 + l], dst.at[me_e], s_sem(k * 2 + l), r_sem(back), at_yz(k, l))

    def input_part(j):
        got(dgn.at[j], dg_r.at[j])

        def cols_b(n, _):
            c = pl.ds(pl.multiple_of(n * 256, 256), 256)
            r = dot(dgu[0], wown[0, j, c, :], NT)
            r += dot(dgu[1], wown[1, j, c, :], NT)
            r += dot(dgn[j, 0], wn[j, 0, c, :], NT)
            r += dot(dgn[j, 1], wn[j, 1, c, :], NT)
            rbb[j, :, :, c] = r.astype(BF).reshape(E, T, 256)
            return 0

        lax.fori_loop(0, Q // 256, cols_b, 0)

    def slot_rows(k):
        return pl.ds(pl.multiple_of((x + k) % 4 * S, S), S)

    def unplace(src, table, dst):
        def one(d, _):
            rows = src[:, pl.ds(pl.multiple_of((x + d) % 4 * S, S), S), :].reshape(E * S, Q)
            dst(d)[...] = dot(table[d], rows).astype(BF)
            return 0

        lax.fori_loop(0, 4, one, 0)

    outs = []
    swap_weights(0, gate_w)
    for q in range(4):
        post(fwd_src.at[:, pl.ds(q * Q, Q)], arr.at[q], pipe_s.at[1, q], pipe_r.at[1, q], at_pipe(1))
    for q in range(4):
        post(grad_src.at[:, pl.ds(q * Q, Q)], inc.at[q], pipe_s.at[0, q], pipe_r.at[0, q], at_pipe(3))

    for q in range(4):
        gain[q] = gain_row[:, q * Q : (q + 1) * Q].astype(F32)
    for c in load_bi:
        c.wait()
    rms_norm(bi, nb, 0)
    nb_sends = spread_half(0, nb, xb, xb_s, xb_r)
    nb_sends += spread_half(1, nb, xb, xb_s, xb_r)
    swap_weights(1, up_w)
    for i, w in enumerate((gate_w, up_w)):
        local(w.at[qa(x)], wown.at[i, 0], ld.at[4 + 2 * i])
        local(w.at[qb(x)], wown.at[i, 1], ld.at[5 + 2 * i])
    load_beo = [local(bwd_expert_out.at[:, pl.ds(q * Q, Q)], beo.at[q], ld.at[9 + q]) for q in range(4)]
    local(down_w.at[:, cols(x)], wd.at[0], ld.at[8])

    route_weight(nb, 4, 1)

    for k in (1, 2, 3):
        got(ptb.at[4 - k], pt_r.at[0, 4 - k])
        got(ptf.at[4 - k], pt_r.at[1, 4 - k])

    yb_sends = [dispatch_half(0, xb, ptb, sbh, rbb, xb_r, yb_s, yb_r)]
    yb_sends.append(dispatch_half(1, xb, ptb, sbh, rbb, xb_r, yb_s, yb_r))
    for q in range(4):
        got(arr.at[q], pipe_r.at[1, q])
    rms_norm(arr, nf, None)
    nf_sends = spread_half(0, nf, xf, xf_s, xf_r) + spread_half(1, nf, xf, xf_s, xf_r)
    for q in range(4):
        got(inc.at[q], pipe_r.at[0, q])
    local(inc.at[x], xi.at[0], xi_r.at[0])
    for k in (1, 3, 2):
        post(inc.at[(x + k) % 4], xi.at[4 - k], xi_s.at[k], xi_r.at[4 - k], at_x(k))

    for k in (1, 3, 2):
        post(down_w.at[:, cols((x + k) % 4)], wd.at[4 - k], wd_s.at[k], wd_r.at[4 - k], at_x(k))

    for c in load_beo:
        c.wait()

    def agree(i, _):
        r = pl.ds(pl.multiple_of(i * 16, 16), 16)
        total = jnp.zeros((16, 1), F32)
        for q in range(4):
            total += jnp.sum(inc[q, r, :].astype(F32) * beo[q, r, :].astype(F32), axis=1, keepdims=True)
        col[3, r, :] = jnp.broadcast_to(total, (16, 128))
        return 0

    lax.fori_loop(0, 4, agree, 0)

    route_weight(nf, 5, 2)

    got(rbb.at[0, 0], yb_r.at[0, 0])
    for c in yb_sends[0]:
        c.wait_send()
    sends += dispatch_half(0, xf, ptf, sbh, rbf, xf_r, yf_s, yf_r)

    got(rbb.at[1, 0], yb_r.at[0, 1])
    for c in yb_sends[1]:
        c.wait_send()
    sends += dispatch_half(1, xf, ptf, sbh, rbf, xf_r, yf_s, yf_r)

    fill_i = place(lambda d: xi.at[d], ptb, sbi)

    def one_i(d, _):
        got(xi.at[d], xi_r.at[d])
        return fill_i(d, 0)

    lax.fori_loop(0, 4, one_i, 0)
    sends += to_experts(sbi, rbi, lambda o: yi_s.at[o], lambda o: yi_r.at[o])

    for i in range(2):
        for j in range(2):
            got(wn.at[j, i], w_r.at[j, i])
            got(wown.at[i, j], ld.at[4 + 2 * i + j])
    for j in range(2):
        for o in range(1, 8):
            got(rbb.at[j, o], yb_r.at[o, j])
    gate_up(rbb, 0)


    swap_parts(0)
    for j in range(2):
        for o in range(8):
            got(rbf.at[j, o], yf_r.at[o, j])
    gate_up(rbf, 1)
    swap_parts(1)
    for j in range(2):
        got(pr.at[1, j], rs_r.at[1, j])

    def act_f(m, _):
        r = pl.ds(pl.multiple_of(m * 32, 32), 32)
        g = acc[1, 0, r, :] + pr[1, 0, 0, r, :].astype(F32) + pr[1, 1, 0, r, :].astype(F32)
        u = acc[1, 1, r, :] + pr[1, 0, 1, r, :].astype(F32) + pr[1, 1, 1, r, :].astype(F32)
        hid[0, r, :] = (g * jax.nn.sigmoid(g) * u).astype(BF)
        return 0

    lax.fori_loop(0, ROWS // 32, act_f, 0)
    for k in (1, 3, 2):
        post(hid.at[0], hid.at[4 - k], hd_s.at[k], hd_r.at[4 - k], at_x(k))

    got(wd.at[0], ld.at[8])
    for d in (1, 2, 3):
        got(wd.at[d], wd_r.at[d])
    for o in range(8):
        got(rbi.at[o], yi_r.at[o])

    def back_own(m, _):
        r = pl.ds(pl.multiple_of(m * 256, 256), 256)
        bacc[r, :] = dot(rbi[pl.ds(m * 4, 4)].reshape(256, Q), wd[0], NT)
        return 0

    def back_other(n, _):
        d, m = 1 + n // 2, n % 2
        r = pl.ds(pl.multiple_of(m * 256, 256), 256)
        bs[d, r, :] = dot(rbi[pl.ds(m * 4, 4)].reshape(256, Q), wd[d], NT).astype(BF)
        return 0

    lax.fori_loop(0, 6, back_other, 0)
    for k in (1, 3, 2):
        post(bs.at[k], br.at[4 - k], bk_s.at[k], bk_r.at[4 - k], at_x(k))
    lax.fori_loop(0, 2, back_own, 0)

    for d in (1, 2, 3):
        got(hid.at[d], hd_r.at[d])

    def cols_f(n, _):
        c = pl.ds(pl.multiple_of(n * 256, 256), 256)
        r = dot(hid[0], wd[0, :, c])
        for d in (1, 2, 3):
            r += dot(hid[d], wd[d, :, c])
        rbi[:, :, c] = r.astype(BF).reshape(E, T, 256)
        return 0

    lax.fori_loop(0, Q // 256, cols_f, 0)
    back_home(rbi, rrf, lambda o: qf_s.at[o], lambda o: qf_r.at[o])

    for j in range(2):
        got(pr.at[0, j], rs_r.at[0, j])
    for d in (1, 2, 3):
        got(br.at[d], bk_r.at[d])

    def act_b(m, _):
        r = pl.ds(pl.multiple_of(m * 32, 32), 32)
        g = acc[0, 0, r, :] + pr[0, 0, 0, r, :].astype(F32) + pr[0, 1, 0, r, :].astype(F32)
        u = acc[0, 1, r, :] + pr[0, 0, 1, r, :].astype(F32) + pr[0, 1, 1, r, :].astype(F32)
        b = bacc[r, :] + br[1, r, :].astype(F32) + br[2, r, :].astype(F32) + br[3, r, :].astype(F32)
        s = jax.nn.sigmoid(g)
        dgu[0, r, :] = (b * u * s * (1.0 + g * (1.0 - s))).astype(BF)
        dgu[1, r, :] = (b * g * s).astype(BF)
        return 0

    lax.fori_loop(0, ROWS // 32, act_b, 0)
    post(dgu, dgn.at[0], dg_s.at[0], dg_r.at[0], at_x(off_a))
    post(dgu, dgn.at[1], dg_s.at[1], dg_r.at[1], at_x(off_b))

    input_part(1)
    for k in (1, 3, 2):
        post(rbb.at[1, :, slot_rows(k)], gb.at[4 - k], gb_s.at[k], gb_r.at[4 - k], at_x(k))
    input_part(0)
    back_home(rbb.at[0], rrb, lambda o: qb_s.at[o], lambda o: qb_r.at[o])

    for o in range(8):
        got(rrf.at[0], qf_r.at[o])
    unplace(rrf, ptf, lambda d: xi.at[d])
    for k in (1, 3, 2):
        post(xi.at[k], ff.at[4 - k], ff_s.at[k], ff_r.at[4 - k], at_x(k))

    for d in (1, 2, 3):
        got(gb.at[d], gb_r.at[d])

    def sum_b(o, _):
        own = rbb[1, o, slot_rows(0), :].astype(F32)
        gs[o, 0] = (own + gb[2, o].astype(F32)).astype(BF)
        gs[o, 1] = (gb[1, o].astype(F32) + gb[3, o].astype(F32)).astype(BF)
        return 0

    lax.fori_loop(0, E, sum_b, 0)
    back_home(gs, rrc, lambda o: qc_s.at[o], lambda o: qc_r.at[o])

    for o in range(8):
        got(rrb.at[0], qb_r.at[o])
    unplace(rrb, ptb, lambda d: xb.at[d, 0])
    for k in (1, 3, 2):
        post(xb.at[k, 0], fb.at[4 - k], fb_s.at[k], fb_r.at[4 - k], at_x(k))

    for c in nf_sends:
        c.wait_send()
    for d in (1, 2, 3):
        got(ff.at[d], ff_r.at[d])

    def finish_f(i, _):
        r = pl.ds(pl.multiple_of(i * 16, 16), 16)
        weight = col[2, r, 0:1]
        for d in range(4):
            q = (x + d) % 4
            e = (xi[0, r, :] if d == 0 else ff[d, r, :]).astype(F32)
            nf[q, r, :] = (arr[q, r, :].astype(F32) + SCALE * weight * e).astype(BF)
        return 0

    lax.fori_loop(0, 4, finish_f, 0)
    outs += [local(nf.at[q], fwd_out.at[:, pl.ds(q * Q, Q)], out_s.at[1, q]) for q in range(4)]

    for c in nb_sends:
        c.wait_send()
    for o in range(8):
        got(rrc.at[0], qc_r.at[o])
    for j in range(2):
        xb[j, 1] = dot(ptb[0], rrc[:, j].reshape(E * S, Q)).astype(BF)
    for d in (1, 2, 3):
        got(fb.at[d], fb_r.at[d])
    quarters = (
        (qa(x), lambda r: xb[0, 0, r, :].astype(F32) + fb[2, r, :].astype(F32)),
        (qa(x + 1), lambda r: fb[1, r, :].astype(F32) + fb[3, r, :].astype(F32)),
        (qb(x), lambda r: xb[0, 1, r, :].astype(F32)),
        (qb(x + 1), lambda r: xb[1, 1, r, :].astype(F32)),
    )

    def finish_b(i, _):
        r = pl.ds(pl.multiple_of(i * 16, 16), 16)
        inv = col[0, r, 0:1]
        weight = col[1, r, 0:1]
        d_logit = SCALE * col[3, r, 0:1] * weight * (1.0 - weight)
        hot = (lax.broadcasted_iota(jnp.int32, (16, E), 1).astype(F32) == col[4, r, 0:1]).astype(F32).astype(BF)
        total = jnp.zeros((16, 1), F32)
        for q, part in quarters:
            g = part(r)
            dn = SCALE * weight * g + d_logit * dot(hot, router_t[:, cols(q)])
            s = dn * gain[q]
            sg[q, r, :] = s
            total += jnp.sum(s * bi[q, r, :].astype(F32), axis=1, keepdims=True)
        factor = inv * inv * inv * (total * (1.0 / D))
        for q in range(4):
            v = bi[q, r, :].astype(F32)
            o = inc[q, r, :].astype(F32) + (inv * sg[q, r, :] - v * factor)
            nb[q, r, :] = o.astype(BF)
        return 0

    lax.fori_loop(0, 4, finish_b, 0)
    outs += [local(nb.at[q], bwd_out.at[:, pl.ds(q * Q, Q)], out_s.at[0, q]) for q in range(4)]

    for c in sends:
        c.wait_send()
    for c in outs:
        c.wait()


def shards(
    fwd_src, fwd_route, bwd_input, bwd_expert_out, grad_src, bwd_route, norm_gain, router, gate_w, up_w, down_w
):
    hbm = pl.BlockSpec(memory_space=pl.ANY)
    vmem = pl.BlockSpec(memory_space=pltpu.VMEM)
    dma = pltpu.SemaphoreType.DMA

    def buf(*shape, dtype=BF):
        return pltpu.VMEM(shape, dtype)

    scratch = [
        buf(4, T, Q), buf(4, T, Q), buf(4, T, Q), buf(4, T, Q),
        buf(4, T, Q), buf(4, T, Q),
        buf(4, 2, T, Q), buf(4, 2, T, Q), buf(4, T, Q),
        buf(2, E, T, Q), buf(E, T, Q),
        buf(2, E, T, Q), buf(E, T, Q), buf(2, E, T, Q),
        buf(E, T, Q), buf(E, T, Q), buf(E, 2, S, Q),
        buf(4, E, S, Q), buf(E, 2, S, Q),
        buf(4, T, Q), buf(4, T, Q),
        buf(2, 2, Q, H), buf(2, 2, Q, H), buf(4, H, Q),
        buf(4, T, E * S), buf(4, T, E * S),
        buf(2, 2, ROWS, H, dtype=F32), buf(2, 2, 2, ROWS, H), buf(2, 2, 2, ROWS, H),
        buf(ROWS, H, dtype=F32), buf(4, ROWS, H), buf(4, ROWS, H),
        buf(2, ROWS, H), buf(2, 2, ROWS, H), buf(4, ROWS, H),
        buf(4, T, Q, dtype=F32), buf(6, T, 128, dtype=F32), buf(4, 1, Q, dtype=F32),
        dma((16,)), dma((2, 4)), dma((2, 4)), dma((2, 4)), dma((2, 4)),
        dma((2, 2)), dma((2, 2)), dma((4,)), dma((4,)),
        dma((4, 2)), dma((4, 2)), dma((4, 2)), dma((4, 2)), dma((4,)), dma((4,)),
        dma((8, 2)), dma((8, 2)), dma((8,)), dma((8,)), dma((8, 2)), dma((8, 2)),
        dma((2, 2)), dma((2, 2)), dma((4,)), dma((4,)), dma((2,)), dma((2,)), dma((4,)), dma((4,)),
        dma((4,)), dma((4,)), dma((8,)), dma((8,)), dma((8,)), dma((8,)), dma((8,)), dma((8,)),
        dma((4,)), dma((4,)), dma((4,)), dma((4,)), dma((2, 4)),
    ]
    out = jax.ShapeDtypeStruct((T, D), BF)
    fwd_out, bwd_out = pl.pallas_call(
        kernel,
        out_shape=(out, out),
        in_specs=[hbm, vmem, hbm, hbm, hbm, vmem, vmem, vmem, hbm, hbm, hbm],
        out_specs=(hbm, hbm),
        scratch_shapes=scratch,
        compiler_params=pltpu.CompilerParams(
            collective_id=0, has_side_effects=True, vmem_limit_bytes=62 * 1024 * 1024
        ),
        cost_estimate=pl.CostEstimate(
            flops=15_000_000_000, bytes_accessed=20_000_000, transcendentals=400_000
        ),
    )(
        fwd_src[0],
        fwd_route.reshape(1, T),
        bwd_input[0],
        bwd_expert_out[0],
        grad_src[0],
        bwd_route.reshape(1, T),
        norm_gain,
        router[0].T,
        gate_w[0].reshape(4, Q, H),
        up_w[0].reshape(4, Q, H),
        down_w[0],
    )
    return (fwd_out[None], bwd_out[None])


def solution(mesh):
    placed = (
        P("pipe", "expert", None),
        P("pipe", "expert", None),
        P("pipe", "expert", None),
        P("pipe", "expert", None),
        P("pipe", "expert", None),
        P("pipe", "expert", None),
        P("pipe", None),
        P("pipe", None, None),
        P("pipe", None, "expert"),
        P("pipe", None, "expert"),
        P("pipe", "expert", None),
    )
    return jax.shard_map(
        shards,
        mesh=mesh,
        in_specs=placed,
        out_specs=(P("pipe", "expert", None), P("pipe", "expert", None)),
        check_vma=False,
    )
```

```python
import functools

import jax
import jax.numpy as jnp
from jax import lax
from jax.experimental import pallas as pl
from jax.experimental.pallas import tpu as pltpu
from jax.sharding import PartitionSpec as P

MESH = pl.DeviceIdType.MESH
BF = jnp.bfloat16
F32 = jnp.float32

D = 7168
Q = 1792
T = 64
E = 8
S = 16
H = 256
ROWS = E * T
SCALE = 2.5
EPS = 1e-06
NT = (((1,), (1,)), ((), ()))
TN = (((0,), (0,)), ((), ()))

OFFS = ((1, 0), (3, 0), (0, 1), (2, 0), (1, 1), (3, 1), (2, 1))


def dot(a, b, dims=(((1,), (0,)), ((), ()))):
    return lax.dot_general(a, b, dims, preferred_element_type=F32)


def kernel(
    fwd_src, fwd_route, bwd_input, bwd_expert_out, grad_src, bwd_route, gain_row, router_t, gate_w, up_w, down_w,
    fwd_out, bwd_out,
    bi, arr, inc, beo, nb, nf, xb, xf, xi, sbh, sbi, rbb, rbi, rbf, rrb, rrf, rrc, gb, gs, fb, ff,
    wown, wn, wd, ptb, ptf, acc, ps, pr, bacc, bs, br, dgu, dgn, hid, sg, col, gain,
    ld, pipe_s, pipe_r, pt_s, pt_r, w_s, w_r, wd_s, wd_r, xb_s, xb_r, xf_s, xf_r, xi_s, xi_r,
    yb_s, yb_r, yi_s, yi_r, yf_s, yf_r, rs_s, rs_r, bk_s, bk_r, dg_s, dg_r, hd_s, hd_r,
    gb_s, gb_r, qb_s, qb_r, qc_s, qc_r, qf_s, qf_r, fb_s, fb_r, ff_s, ff_r, out_s,
):
    p = lax.axis_index("pipe")
    ei = lax.axis_index("expert")
    me_e = ei // 4
    y, z, x = ei // 8, me_e % 2, ei % 4
    odd = x % 2

    def at_x(k):
        return (p, me_e * 4 + (x + k) % 4)

    def at_yz(k, l):
        return (p, ((y + k) % 4) * 8 + ((z + l) % 2) * 4 + x)

    def expert_at(k, l):
        return ((y + k) % 4) * 2 + (z + l) % 2

    def at_pipe(k):
        return ((p + k) % 4, ei)

    def qa(xx):
        return xx % 2

    def qb(xx):
        return 3 - xx % 2

    off_a = 1 + 2 * odd
    off_b = 3 - 2 * odd

    sends = []

    def put(src, dst, s_sem, r_sem, device):
        c = pltpu.make_async_remote_copy(
            src_ref=src, dst_ref=dst, send_sem=s_sem, recv_sem=r_sem, device_id=device, device_id_type=MESH
        )
        c.start()
        return c

    def post(*args):
        sends.append(put(*args))

    def got(ref, sem):
        pltpu.make_async_copy(ref, ref, sem).wait()

    def local(src, dst, sem):
        c = pltpu.make_async_copy(src, dst, sem)
        c.start()
        return c

    def cols(q):
        return pl.ds(pl.multiple_of(q * Q, 128), Q)

    load_bi = [local(bwd_input.at[:, pl.ds(q * Q, Q)], bi.at[q], ld.at[q]) for q in range(4)]

    barrier = pltpu.get_barrier_semaphore()
    peers = [at_x(k) for k in (1, 2, 3)] + [at_yz(k, l) for k, l in OFFS] + [at_pipe(1), at_pipe(3)]
    for peer in peers:
        pl.semaphore_signal(barrier, inc=1, device_id=peer, device_id_type=MESH)
    pl.semaphore_wait(barrier, len(peers))

    def swap_weights(i, w):
        post(w.at[qa(x + 1)], wn.at[0, i], w_s.at[0, i], w_r.at[0, i], at_x(off_a))
        post(w.at[qb(x + 1)], wn.at[1, i], w_s.at[1, i], w_r.at[1, i], at_x(off_b))

    def slots(route, table, keep):
        row = lax.broadcasted_iota(jnp.int32, (T, T), 0)
        lower = lax.broadcasted_iota(jnp.int32, (T, T), 1)
        eye = (row == lower).astype(F32)
        chosen = jnp.sum(eye * route[...].astype(F32), axis=1, keepdims=True)
        col[keep] = jnp.broadcast_to(chosen, (T, 128))
        lane = lax.broadcasted_iota(jnp.int32, (T, E * S), 1).astype(F32)
        hot = (lane == chosen).astype(F32)
        low = (row > lower).astype(F32)
        prior = dot(low.astype(BF), hot.astype(BF))
        rank = jnp.sum(prior * hot, axis=1, keepdims=True)
        table[0] = (lane == chosen * S + rank).astype(F32).astype(BF)

    slots(bwd_route, ptb, 4)
    slots(fwd_route, ptf, 5)
    for i, table in enumerate((ptb, ptf)):
        for k in (1, 2, 3):
            post(table.at[0], table.at[4 - k], pt_s.at[i, k], pt_r.at[i, 4 - k], at_x(k))

    def rms_norm(v, normed, keep):
        def rows(i, _):
            r = pl.ds(pl.multiple_of(i * 16, 16), 16)
            total = jnp.zeros((16, 1), F32)
            for q in range(4):
                w = v[q, r, :].astype(F32)
                total += jnp.sum(w * w, axis=1, keepdims=True)
            inv = lax.rsqrt(total * (1.0 / D) + EPS)
            if keep is not None:
                col[keep, r, :] = jnp.broadcast_to(inv, (16, 128))
            for q in range(4):
                normed[q, r, :] = (v[q, r, :].astype(F32) * inv * gain[q]).astype(BF)
            return 0

        lax.fori_loop(0, 4, rows, 0)

    def route_weight(normed, chosen, keep):
        logits = jnp.zeros((T, E), F32)
        for q in range(4):
            logits += dot(normed[q], router_t[:, q * Q : (q + 1) * Q], NT)
        hot = (lax.broadcasted_iota(jnp.int32, (T, E), 1).astype(F32) == col[chosen, :, 0:1]).astype(F32)
        weight = jax.nn.sigmoid(jnp.sum(logits * hot, axis=1, keepdims=True))
        col[keep] = jnp.broadcast_to(weight, (T, 128))

    def spread_half(j, normed, xs, s_sem, r_sem):
        quarter = (qa, qb)[j]
        local(normed.at[quarter(x)], xs.at[0, j], r_sem.at[0, j])
        return [
            put(normed.at[quarter(x + k)], xs.at[4 - k, j], s_sem.at[k, j], r_sem.at[4 - k, j], at_x(k))
            for k in (1, 3, 2)
        ]

    def place(block, table, dst):
        def one(d, _):
            r = dot(table[d], block(d)[...], TN).astype(BF).reshape(E, S, Q)
            dst[:, pl.ds(pl.multiple_of((x + d) % 4 * S, S), S), :] = r
            return 0

        return one

    def to_experts(src, dst, s_sem, r_sem):
        local(src.at[me_e], dst.at[0], r_sem(0))
        out = []
        for k, l in OFFS:
            back = ((4 - k) % 4) * 2 + l
            out.append(put(src.at[expert_at(k, l)], dst.at[back], s_sem(k * 2 + l), r_sem(back), at_yz(k, l)))
        return out

    def dispatch_half(j, xs, table, sb, rb, xr, ys, yr):
        fill = place(lambda d: xs.at[d, j], table, sb.at[j])

        def one(d, _):
            got(xs.at[d, j], xr.at[d, j])
            return fill(d, 0)

        lax.fori_loop(0, 4, one, 0)
        return to_experts(sb.at[j], rb.at[j], lambda o: ys.at[o, j], lambda o: yr.at[o, j])

    def gate_up(rb, i):
        def one(n, _):
            w, m = n // 2, n % 2
            r = pl.ds(pl.multiple_of(m * 256, 256), 256)
            m4 = pl.ds(m * 4, 4)
            ra = rb[0, m4].reshape(256, Q)
            acc[i, w, r, :] = dot(ra, wown[w, 0])
            ps[i, 0, w, r, :] = dot(ra, wn[0, w]).astype(BF)
            rc = rb[1, m4].reshape(256, Q)
            acc[i, w, r, :] += dot(rc, wown[w, 1])
            ps[i, 1, w, r, :] = dot(rc, wn[1, w]).astype(BF)
            return 0

        lax.fori_loop(0, 4, one, 0)

    def swap_parts(i):
        post(ps.at[i, 0], pr.at[i, 0], rs_s.at[i, 0], rs_r.at[i, 0], at_x(off_a))
        post(ps.at[i, 1], pr.at[i, 1], rs_s.at[i, 1], rs_r.at[i, 1], at_x(off_b))

    def back_home(src, dst, s_sem, r_sem):
        local(src.at[0], dst.at[me_e], r_sem(0))
        for k, l in OFFS:
            back = ((4 - k) % 4) * 2 + l
            post(src.at[k * 2 + l], dst.at[me_e], s_sem(k * 2 + l), r_sem(back), at_yz(k, l))

    def input_part(j):
        got(dgn.at[j], dg_r.at[j])

        def cols_b(n, _):
            c = pl.ds(pl.multiple_of(n * 256, 256), 256)
            r = dot(dgu[0], wown[0, j, c, :], NT)
            r += dot(dgu[1], wown[1, j, c, :], NT)
            r += dot(dgn[j, 0], wn[j, 0, c, :], NT)
            r += dot(dgn[j, 1], wn[j, 1, c, :], NT)
            rbb[j, :, :, c] = r.astype(BF).reshape(E, T, 256)
            return 0

        lax.fori_loop(0, Q // 256, cols_b, 0)

    def slot_rows(k):
        return pl.ds(pl.multiple_of((x + k) % 4 * S, S), S)

    def unplace(src, table, dst):
        def one(d, _):
            rows = src[:, pl.ds(pl.multiple_of((x + d) % 4 * S, S), S), :].reshape(E * S, Q)
            dst(d)[...] = dot(table[d], rows).astype(BF)
            return 0

        lax.fori_loop(0, 4, one, 0)

    outs = []
    swap_weights(0, gate_w)
    for q in range(4):
        post(fwd_src.at[:, pl.ds(q * Q, Q)], arr.at[q], pipe_s.at[1, q], pipe_r.at[1, q], at_pipe(1))
    for q in range(4):
        post(grad_src.at[:, pl.ds(q * Q, Q)], inc.at[q], pipe_s.at[0, q], pipe_r.at[0, q], at_pipe(3))

    for q in range(4):
        gain[q] = gain_row[:, q * Q : (q + 1) * Q].astype(F32)
    for c in load_bi:
        c.wait()
    rms_norm(bi, nb, 0)
    nb_sends = spread_half(0, nb, xb, xb_s, xb_r)
    nb_sends += spread_half(1, nb, xb, xb_s, xb_r)
    swap_weights(1, up_w)
    for i, w in enumerate((gate_w, up_w)):
        local(w.at[qa(x)], wown.at[i, 0], ld.at[4 + 2 * i])
        local(w.at[qb(x)], wown.at[i, 1], ld.at[5 + 2 * i])
    load_beo = [local(bwd_expert_out.at[:, pl.ds(q * Q, Q)], beo.at[q], ld.at[9 + q]) for q in range(4)]
    local(down_w.at[:, cols(x)], wd.at[0], ld.at[8])

    route_weight(nb, 4, 1)

    for k in (1, 2, 3):
        got(ptb.at[4 - k], pt_r.at[0, 4 - k])
        got(ptf.at[4 - k], pt_r.at[1, 4 - k])

    yb_sends = [dispatch_half(0, xb, ptb, sbh, rbb, xb_r, yb_s, yb_r)]
    yb_sends.append(dispatch_half(1, xb, ptb, sbh, rbb, xb_r, yb_s, yb_r))
    for q in range(4):
        got(arr.at[q], pipe_r.at[1, q])
    rms_norm(arr, nf, None)
    nf_sends = spread_half(0, nf, xf, xf_s, xf_r) + spread_half(1, nf, xf, xf_s, xf_r)
    for q in range(4):
        got(inc.at[q], pipe_r.at[0, q])
    local(inc.at[x], xi.at[0], xi_r.at[0])
    for k in (1, 3, 2):
        post(inc.at[(x + k) % 4], xi.at[4 - k], xi_s.at[k], xi_r.at[4 - k], at_x(k))

    for c in load_beo:
        c.wait()

    def agree(i, _):
        r = pl.ds(pl.multiple_of(i * 16, 16), 16)
        total = jnp.zeros((16, 1), F32)
        for q in range(4):
            total += jnp.sum(inc[q, r, :].astype(F32) * beo[q, r, :].astype(F32), axis=1, keepdims=True)
        col[3, r, :] = jnp.broadcast_to(total, (16, 128))
        return 0

    lax.fori_loop(0, 4, agree, 0)

    route_weight(nf, 5, 2)

    got(rbb.at[0, 0], yb_r.at[0, 0])
    for c in yb_sends[0]:
        c.wait_send()
    sends += dispatch_half(0, xf, ptf, sbh, rbf, xf_r, yf_s, yf_r)

    got(rbb.at[1, 0], yb_r.at[0, 1])
    for c in yb_sends[1]:
        c.wait_send()
    sends += dispatch_half(1, xf, ptf, sbh, rbf, xf_r, yf_s, yf_r)

    for k in (1, 3, 2):
        post(down_w.at[:, cols((x + k) % 4)], wd.at[4 - k], wd_s.at[k], wd_r.at[4 - k], at_x(k))

    fill_i = place(lambda d: xi.at[d], ptb, sbi)

    def one_i(d, _):
        got(xi.at[d], xi_r.at[d])
        return fill_i(d, 0)

    lax.fori_loop(0, 4, one_i, 0)
    sends += to_experts(sbi, rbi, lambda o: yi_s.at[o], lambda o: yi_r.at[o])

    for i in range(2):
        for j in range(2):
            got(wn.at[j, i], w_r.at[j, i])
            got(wown.at[i, j], ld.at[4 + 2 * i + j])
    for j in range(2):
        for o in range(1, 8):
            got(rbb.at[j, o], yb_r.at[o, j])
    gate_up(rbb, 0)


    swap_parts(0)
    for j in range(2):
        for o in range(8):
            got(rbf.at[j, o], yf_r.at[o, j])
    gate_up(rbf, 1)
    swap_parts(1)
    for j in range(2):
        got(pr.at[1, j], rs_r.at[1, j])

    def act_f(m, _):
        r = pl.ds(pl.multiple_of(m * 32, 32), 32)
        g = acc[1, 0, r, :] + pr[1, 0, 0, r, :].astype(F32) + pr[1, 1, 0, r, :].astype(F32)
        u = acc[1, 1, r, :] + pr[1, 0, 1, r, :].astype(F32) + pr[1, 1, 1, r, :].astype(F32)
        hid[0, r, :] = (g * jax.nn.sigmoid(g) * u).astype(BF)
        return 0

    lax.fori_loop(0, ROWS // 32, act_f, 0)
    for k in (1, 3, 2):
        post(hid.at[0], hid.at[4 - k], hd_s.at[k], hd_r.at[4 - k], at_x(k))

    got(wd.at[0], ld.at[8])
    for d in (1, 2, 3):
        got(wd.at[d], wd_r.at[d])
    for o in range(8):
        got(rbi.at[o], yi_r.at[o])

    def back_own(m, _):
        r = pl.ds(pl.multiple_of(m * 256, 256), 256)
        bacc[r, :] = dot(rbi[pl.ds(m * 4, 4)].reshape(256, Q), wd[0], NT)
        return 0

    def back_other(n, _):
        d, m = 1 + n // 2, n % 2
        r = pl.ds(pl.multiple_of(m * 256, 256), 256)
        bs[d, r, :] = dot(rbi[pl.ds(m * 4, 4)].reshape(256, Q), wd[d], NT).astype(BF)
        return 0

    lax.fori_loop(0, 6, back_other, 0)
    for k in (1, 3, 2):
        post(bs.at[k], br.at[4 - k], bk_s.at[k], bk_r.at[4 - k], at_x(k))
    lax.fori_loop(0, 2, back_own, 0)

    for d in (1, 2, 3):
        got(hid.at[d], hd_r.at[d])

    def cols_f(n, _):
        c = pl.ds(pl.multiple_of(n * 256, 256), 256)
        r = dot(hid[0], wd[0, :, c])
        for d in (1, 2, 3):
            r += dot(hid[d], wd[d, :, c])
        rbi[:, :, c] = r.astype(BF).reshape(E, T, 256)
        return 0

    lax.fori_loop(0, Q // 256, cols_f, 0)
    back_home(rbi, rrf, lambda o: qf_s.at[o], lambda o: qf_r.at[o])

    for j in range(2):
        got(pr.at[0, j], rs_r.at[0, j])
    for d in (1, 2, 3):
        got(br.at[d], bk_r.at[d])

    def act_b(m, _):
        r = pl.ds(pl.multiple_of(m * 32, 32), 32)
        g = acc[0, 0, r, :] + pr[0, 0, 0, r, :].astype(F32) + pr[0, 1, 0, r, :].astype(F32)
        u = acc[0, 1, r, :] + pr[0, 0, 1, r, :].astype(F32) + pr[0, 1, 1, r, :].astype(F32)
        b = bacc[r, :] + br[1, r, :].astype(F32) + br[2, r, :].astype(F32) + br[3, r, :].astype(F32)
        s = jax.nn.sigmoid(g)
        dgu[0, r, :] = (b * u * s * (1.0 + g * (1.0 - s))).astype(BF)
        dgu[1, r, :] = (b * g * s).astype(BF)
        return 0

    lax.fori_loop(0, ROWS // 32, act_b, 0)
    post(dgu, dgn.at[0], dg_s.at[0], dg_r.at[0], at_x(off_a))
    post(dgu, dgn.at[1], dg_s.at[1], dg_r.at[1], at_x(off_b))

    input_part(1)
    for k in (1, 3, 2):
        post(rbb.at[1, :, slot_rows(k)], gb.at[4 - k], gb_s.at[k], gb_r.at[4 - k], at_x(k))
    input_part(0)
    back_home(rbb.at[0], rrb, lambda o: qb_s.at[o], lambda o: qb_r.at[o])

    for o in range(8):
        got(rrf.at[0], qf_r.at[o])
    unplace(rrf, ptf, lambda d: xi.at[d])
    for k in (1, 3, 2):
        post(xi.at[k], ff.at[4 - k], ff_s.at[k], ff_r.at[4 - k], at_x(k))

    for d in (1, 2, 3):
        got(gb.at[d], gb_r.at[d])

    def sum_b(o, _):
        own = rbb[1, o, slot_rows(0), :].astype(F32)
        gs[o, 0] = (own + gb[2, o].astype(F32)).astype(BF)
        gs[o, 1] = (gb[1, o].astype(F32) + gb[3, o].astype(F32)).astype(BF)
        return 0

    lax.fori_loop(0, E, sum_b, 0)
    back_home(gs, rrc, lambda o: qc_s.at[o], lambda o: qc_r.at[o])

    for o in range(8):
        got(rrb.at[0], qb_r.at[o])
    unplace(rrb, ptb, lambda d: xb.at[d, 0])
    for k in (1, 3, 2):
        post(xb.at[k, 0], fb.at[4 - k], fb_s.at[k], fb_r.at[4 - k], at_x(k))

    for c in nf_sends:
        c.wait_send()
    for d in (1, 2, 3):
        got(ff.at[d], ff_r.at[d])

    def finish_f(i, _):
        r = pl.ds(pl.multiple_of(i * 16, 16), 16)
        weight = col[2, r, 0:1]
        for d in range(4):
            q = (x + d) % 4
            e = (xi[0, r, :] if d == 0 else ff[d, r, :]).astype(F32)
            nf[q, r, :] = (arr[q, r, :].astype(F32) + SCALE * weight * e).astype(BF)
        return 0

    lax.fori_loop(0, 4, finish_f, 0)
    outs += [local(nf.at[q], fwd_out.at[:, pl.ds(q * Q, Q)], out_s.at[1, q]) for q in range(4)]

    for c in nb_sends:
        c.wait_send()
    for o in range(8):
        got(rrc.at[0], qc_r.at[o])
    for j in range(2):
        xb[j, 1] = dot(ptb[0], rrc[:, j].reshape(E * S, Q)).astype(BF)
    for d in (1, 2, 3):
        got(fb.at[d], fb_r.at[d])
    quarters = (
        (qa(x), lambda r: xb[0, 0, r, :].astype(F32) + fb[2, r, :].astype(F32)),
        (qa(x + 1), lambda r: fb[1, r, :].astype(F32) + fb[3, r, :].astype(F32)),
        (qb(x), lambda r: xb[0, 1, r, :].astype(F32)),
        (qb(x + 1), lambda r: xb[1, 1, r, :].astype(F32)),
    )

    def finish_b(i, _):
        r = pl.ds(pl.multiple_of(i * 16, 16), 16)
        inv = col[0, r, 0:1]
        weight = col[1, r, 0:1]
        d_logit = SCALE * col[3, r, 0:1] * weight * (1.0 - weight)
        hot = (lax.broadcasted_iota(jnp.int32, (16, E), 1).astype(F32) == col[4, r, 0:1]).astype(F32).astype(BF)
        total = jnp.zeros((16, 1), F32)
        for q, part in quarters:
            g = part(r)
            dn = SCALE * weight * g + d_logit * dot(hot, router_t[:, cols(q)])
            s = dn * gain[q]
            sg[q, r, :] = s
            total += jnp.sum(s * bi[q, r, :].astype(F32), axis=1, keepdims=True)
        factor = inv * inv * inv * (total * (1.0 / D))
        for q in range(4):
            v = bi[q, r, :].astype(F32)
            o = inc[q, r, :].astype(F32) + (inv * sg[q, r, :] - v * factor)
            nb[q, r, :] = o.astype(BF)
        return 0

    lax.fori_loop(0, 4, finish_b, 0)
    outs += [local(nb.at[q], bwd_out.at[:, pl.ds(q * Q, Q)], out_s.at[0, q]) for q in range(4)]

    for c in sends:
        c.wait_send()
    for c in outs:
        c.wait()


def hand_out(fwd_in, bwd_in, fwd_out, bwd_out):
    fwd_out[...] = fwd_in[...]
    bwd_out[...] = bwd_in[...]


def shards(
    fwd_src, fwd_route, bwd_input, bwd_expert_out, grad_src, bwd_route, norm_gain, router, gate_w, up_w, down_w
):
    hbm = pl.BlockSpec(memory_space=pl.ANY)
    vmem = pl.BlockSpec(memory_space=pltpu.VMEM)
    dma = pltpu.SemaphoreType.DMA

    def buf(*shape, dtype=BF):
        return pltpu.VMEM(shape, dtype)

    scratch = [
        buf(4, T, Q), buf(4, T, Q), buf(4, T, Q), buf(4, T, Q),
        buf(4, T, Q), buf(4, T, Q),
        buf(4, 2, T, Q), buf(4, 2, T, Q), buf(4, T, Q),
        buf(2, E, T, Q), buf(E, T, Q),
        buf(2, E, T, Q), buf(E, T, Q), buf(2, E, T, Q),
        buf(E, T, Q), buf(E, T, Q), buf(E, 2, S, Q),
        buf(4, E, S, Q), buf(E, 2, S, Q),
        buf(4, T, Q), buf(4, T, Q),
        buf(2, 2, Q, H), buf(2, 2, Q, H), buf(4, H, Q),
        buf(4, T, E * S), buf(4, T, E * S),
        buf(2, 2, ROWS, H, dtype=F32), buf(2, 2, 2, ROWS, H), buf(2, 2, 2, ROWS, H),
        buf(ROWS, H, dtype=F32), buf(4, ROWS, H), buf(4, ROWS, H),
        buf(2, ROWS, H), buf(2, 2, ROWS, H), buf(4, ROWS, H),
        buf(4, T, Q, dtype=F32), buf(6, T, 128, dtype=F32), buf(4, 1, Q, dtype=F32),
        dma((16,)), dma((2, 4)), dma((2, 4)), dma((2, 4)), dma((2, 4)),
        dma((2, 2)), dma((2, 2)), dma((4,)), dma((4,)),
        dma((4, 2)), dma((4, 2)), dma((4, 2)), dma((4, 2)), dma((4,)), dma((4,)),
        dma((8, 2)), dma((8, 2)), dma((8,)), dma((8,)), dma((8, 2)), dma((8, 2)),
        dma((2, 2)), dma((2, 2)), dma((4,)), dma((4,)), dma((2,)), dma((2,)), dma((4,)), dma((4,)),
        dma((4,)), dma((4,)), dma((8,)), dma((8,)), dma((8,)), dma((8,)), dma((8,)), dma((8,)),
        dma((4,)), dma((4,)), dma((4,)), dma((4,)), dma((2, 4)),
    ]
    out = jax.ShapeDtypeStruct((T, D), BF)
    fwd_out, bwd_out = pl.pallas_call(
        kernel,
        out_shape=(out, out),
        in_specs=[hbm, vmem, hbm, hbm, hbm, vmem, vmem, vmem, hbm, hbm, hbm],
        out_specs=(hbm, hbm),
        scratch_shapes=scratch,
        compiler_params=pltpu.CompilerParams(
            collective_id=0, has_side_effects=True, vmem_limit_bytes=62 * 1024 * 1024
        ),
        cost_estimate=pl.CostEstimate(
            flops=15_000_000_000, bytes_accessed=20_000_000, transcendentals=400_000
        ),
    )(
        fwd_src[0],
        fwd_route.reshape(1, T),
        bwd_input[0],
        bwd_expert_out[0],
        grad_src[0],
        bwd_route.reshape(1, T),
        norm_gain,
        router[0].T,
        gate_w[0].reshape(4, Q, H),
        up_w[0].reshape(4, Q, H),
        down_w[0],
    )
    rows = pl.BlockSpec((32, D), lambda i: (i, 0))
    fwd_out, bwd_out = pl.pallas_call(
        hand_out,
        out_shape=(out, out),
        grid=(2,),
        in_specs=[rows, rows],
        out_specs=(rows, rows),
    )(fwd_out, bwd_out)
    return (fwd_out[None], bwd_out[None])


def solution(mesh):
    placed = (
        P("pipe", "expert", None),
        P("pipe", "expert", None),
        P("pipe", "expert", None),
        P("pipe", "expert", None),
        P("pipe", "expert", None),
        P("pipe", "expert", None),
        P("pipe", None),
        P("pipe", None, None),
        P("pipe", None, "expert"),
        P("pipe", None, "expert"),
        P("pipe", "expert", None),
    )
    return jax.shard_map(
        shards,
        mesh=mesh,
        in_specs=placed,
        out_specs=(P("pipe", "expert", None), P("pipe", "expert", None)),
        check_vma=False,
    )
```

```python
import functools

import jax
import jax.numpy as jnp
from jax import lax
from jax.experimental import pallas as pl
from jax.experimental.pallas import tpu as pltpu
from jax.sharding import PartitionSpec as P

MESH = pl.DeviceIdType.MESH
BF = jnp.bfloat16
F32 = jnp.float32

D = 7168
Q = 1792
T = 64
E = 8
S = 16
H = 256
ROWS = E * T
SCALE = 2.5
EPS = 1e-06
NT = (((1,), (1,)), ((), ()))
TN = (((0,), (0,)), ((), ()))

OFFS = ((1, 0), (3, 0), (0, 1), (2, 0), (1, 1), (3, 1), (2, 1))


def dot(a, b, dims=(((1,), (0,)), ((), ()))):
    return lax.dot_general(a, b, dims, preferred_element_type=F32)


def kernel(
    fwd_src, fwd_route, bwd_input, bwd_expert_out, grad_src, bwd_route, gain_row, router_t, gate_w, up_w, down_w,
    fwd_out, bwd_out,
    bi, arr, inc, beo, nb, nf, xb, xf, xi, sbh, sbi, rbb, rbi, rbf, rrb, rrf, rrc, gb, gs, fb, ff,
    wown, wn, wd, ptb, ptf, acc, ps, pr, bacc, bs, br, dgu, dgn, hid, sg, col, gain,
    ld, pipe_s, pipe_r, pt_s, pt_r, w_s, w_r, wd_s, wd_r, xb_s, xb_r, xf_s, xf_r, xi_s, xi_r,
    yb_s, yb_r, yi_s, yi_r, yf_s, yf_r, rs_s, rs_r, bk_s, bk_r, dg_s, dg_r, hd_s, hd_r,
    gb_s, gb_r, qb_s, qb_r, qc_s, qc_r, qf_s, qf_r, fb_s, fb_r, ff_s, ff_r, out_s,
):
    p = lax.axis_index("pipe")
    ei = lax.axis_index("expert")
    me_e = ei // 4
    y, z, x = ei // 8, me_e % 2, ei % 4
    odd = x % 2

    def at_x(k):
        return (p, me_e * 4 + (x + k) % 4)

    def at_yz(k, l):
        return (p, ((y + k) % 4) * 8 + ((z + l) % 2) * 4 + x)

    def expert_at(k, l):
        return ((y + k) % 4) * 2 + (z + l) % 2

    def at_pipe(k):
        return ((p + k) % 4, ei)

    def qa(xx):
        return xx % 2

    def qb(xx):
        return 3 - xx % 2

    off_a = 1 + 2 * odd
    off_b = 3 - 2 * odd

    sends = []

    def put(src, dst, s_sem, r_sem, device):
        c = pltpu.make_async_remote_copy(
            src_ref=src, dst_ref=dst, send_sem=s_sem, recv_sem=r_sem, device_id=device, device_id_type=MESH
        )
        c.start()
        return c

    def post(*args):
        sends.append(put(*args))

    def got(ref, sem):
        pltpu.make_async_copy(ref, ref, sem).wait()

    def local(src, dst, sem):
        c = pltpu.make_async_copy(src, dst, sem)
        c.start()
        return c

    def cols(q):
        return pl.ds(pl.multiple_of(q * Q, 128), Q)

    load_bi = [local(bwd_input.at[:, pl.ds(q * Q, Q)], bi.at[q], ld.at[q]) for q in range(4)]

    barrier = pltpu.get_barrier_semaphore()
    peers = [at_x(k) for k in (1, 2, 3)] + [at_yz(k, l) for k, l in OFFS] + [at_pipe(1), at_pipe(3)]
    for peer in peers:
        pl.semaphore_signal(barrier, inc=1, device_id=peer, device_id_type=MESH)
    pl.semaphore_wait(barrier, len(peers))

    def swap_weights(i, w):
        post(w.at[qa(x + 1)], wn.at[0, i], w_s.at[0, i], w_r.at[0, i], at_x(off_a))
        post(w.at[qb(x + 1)], wn.at[1, i], w_s.at[1, i], w_r.at[1, i], at_x(off_b))

    def slots(route, table, keep):
        row = lax.broadcasted_iota(jnp.int32, (T, T), 0)
        lower = lax.broadcasted_iota(jnp.int32, (T, T), 1)
        eye = (row == lower).astype(F32)
        chosen = jnp.sum(eye * route[...].astype(F32), axis=1, keepdims=True)
        col[keep] = jnp.broadcast_to(chosen, (T, 128))
        lane = lax.broadcasted_iota(jnp.int32, (T, E * S), 1).astype(F32)
        hot = (lane == chosen).astype(F32)
        low = (row > lower).astype(F32)
        prior = dot(low.astype(BF), hot.astype(BF))
        rank = jnp.sum(prior * hot, axis=1, keepdims=True)
        table[0] = (lane == chosen * S + rank).astype(F32).astype(BF)

    slots(bwd_route, ptb, 4)
    slots(fwd_route, ptf, 5)
    for i, table in enumerate((ptb, ptf)):
        for k in (1, 2, 3):
            post(table.at[0], table.at[4 - k], pt_s.at[i, k], pt_r.at[i, 4 - k], at_x(k))

    def rms_norm(v, normed, keep):
        def rows(i, _):
            r = pl.ds(pl.multiple_of(i * 16, 16), 16)
            total = jnp.zeros((16, 1), F32)
            for q in range(4):
                w = v[q, r, :].astype(F32)
                total += jnp.sum(w * w, axis=1, keepdims=True)
            inv = lax.rsqrt(total * (1.0 / D) + EPS)
            if keep is not None:
                col[keep, r, :] = jnp.broadcast_to(inv, (16, 128))
            for q in range(4):
                normed[q, r, :] = (v[q, r, :].astype(F32) * inv * gain[q]).astype(BF)
            return 0

        lax.fori_loop(0, 4, rows, 0)

    def route_weight(normed, chosen, keep):
        logits = jnp.zeros((T, E), F32)
        for q in range(4):
            logits += dot(normed[q], router_t[:, q * Q : (q + 1) * Q], NT)
        hot = (lax.broadcasted_iota(jnp.int32, (T, E), 1).astype(F32) == col[chosen, :, 0:1]).astype(F32)
        weight = jax.nn.sigmoid(jnp.sum(logits * hot, axis=1, keepdims=True))
        col[keep] = jnp.broadcast_to(weight, (T, 128))

    def spread_half(j, normed, xs, s_sem, r_sem):
        quarter = (qa, qb)[j]
        local(normed.at[quarter(x)], xs.at[0, j], r_sem.at[0, j])
        return [
            put(normed.at[quarter(x + k)], xs.at[4 - k, j], s_sem.at[k, j], r_sem.at[4 - k, j], at_x(k))
            for k in (1, 3, 2)
        ]

    def place(block, table, dst):
        def one(d, _):
            r = dot(table[d], block(d)[...], TN).astype(BF).reshape(E, S, Q)
            dst[:, pl.ds(pl.multiple_of((x + d) % 4 * S, S), S), :] = r
            return 0

        return one

    def to_experts(src, dst, s_sem, r_sem):
        local(src.at[me_e], dst.at[0], r_sem(0))
        out = []
        for k, l in OFFS:
            back = ((4 - k) % 4) * 2 + l
            out.append(put(src.at[expert_at(k, l)], dst.at[back], s_sem(k * 2 + l), r_sem(back), at_yz(k, l)))
        return out

    def dispatch_half(j, xs, table, sb, rb, xr, ys, yr):
        fill = place(lambda d: xs.at[d, j], table, sb.at[j])

        def one(d, _):
            got(xs.at[d, j], xr.at[d, j])
            return fill(d, 0)

        lax.fori_loop(0, 4, one, 0)
        return to_experts(sb.at[j], rb.at[j], lambda o: ys.at[o, j], lambda o: yr.at[o, j])

    def gate_up(rb, i):
        def others(n, _):
            w, m = n // 2, n % 2
            r = pl.ds(pl.multiple_of(m * 256, 256), 256)
            m4 = pl.ds(m * 4, 4)
            ps[i, 0, w, r, :] = dot(rb[0, m4].reshape(256, Q), wn[0, w]).astype(BF)
            ps[i, 1, w, r, :] = dot(rb[1, m4].reshape(256, Q), wn[1, w]).astype(BF)
            return 0

        def own(n, _):
            w, m = n // 2, n % 2
            r = pl.ds(pl.multiple_of(m * 256, 256), 256)
            m4 = pl.ds(m * 4, 4)
            acc[i, w, r, :] = dot(rb[0, m4].reshape(256, Q), wown[w, 0])
            acc[i, w, r, :] += dot(rb[1, m4].reshape(256, Q), wown[w, 1])
            return 0

        lax.fori_loop(0, 4, others, 0)
        swap_parts(i)
        lax.fori_loop(0, 4, own, 0)

    def swap_parts(i):
        post(ps.at[i, 0], pr.at[i, 0], rs_s.at[i, 0], rs_r.at[i, 0], at_x(off_a))
        post(ps.at[i, 1], pr.at[i, 1], rs_s.at[i, 1], rs_r.at[i, 1], at_x(off_b))

    def back_home(src, dst, s_sem, r_sem):
        local(src.at[0], dst.at[me_e], r_sem(0))
        for k, l in OFFS:
            back = ((4 - k) % 4) * 2 + l
            post(src.at[k * 2 + l], dst.at[me_e], s_sem(k * 2 + l), r_sem(back), at_yz(k, l))

    def input_part(j):
        got(dgn.at[j], dg_r.at[j])

        def cols_b(n, _):
            c = pl.ds(pl.multiple_of(n * 256, 256), 256)
            r = dot(dgu[0], wown[0, j, c, :], NT)
            r += dot(dgu[1], wown[1, j, c, :], NT)
            r += dot(dgn[j, 0], wn[j, 0, c, :], NT)
            r += dot(dgn[j, 1], wn[j, 1, c, :], NT)
            rbb[j, :, :, c] = r.astype(BF).reshape(E, T, 256)
            return 0

        lax.fori_loop(0, Q // 256, cols_b, 0)

    def slot_rows(k):
        return pl.ds(pl.multiple_of((x + k) % 4 * S, S), S)

    def unplace(src, table, dst):
        def one(d, _):
            rows = src[:, pl.ds(pl.multiple_of((x + d) % 4 * S, S), S), :].reshape(E * S, Q)
            dst(d)[...] = dot(table[d], rows).astype(BF)
            return 0

        lax.fori_loop(0, 4, one, 0)

    outs = []
    swap_weights(0, gate_w)
    for q in range(4):
        post(fwd_src.at[:, pl.ds(q * Q, Q)], arr.at[q], pipe_s.at[1, q], pipe_r.at[1, q], at_pipe(1))
    for q in range(4):
        post(grad_src.at[:, pl.ds(q * Q, Q)], inc.at[q], pipe_s.at[0, q], pipe_r.at[0, q], at_pipe(3))

    for q in range(4):
        gain[q] = gain_row[:, q * Q : (q + 1) * Q].astype(F32)
    for c in load_bi:
        c.wait()
    rms_norm(bi, nb, 0)
    nb_sends = spread_half(0, nb, xb, xb_s, xb_r)
    nb_sends += spread_half(1, nb, xb, xb_s, xb_r)
    swap_weights(1, up_w)
    for i, w in enumerate((gate_w, up_w)):
        local(w.at[qa(x)], wown.at[i, 0], ld.at[4 + 2 * i])
        local(w.at[qb(x)], wown.at[i, 1], ld.at[5 + 2 * i])
    load_beo = [local(bwd_expert_out.at[:, pl.ds(q * Q, Q)], beo.at[q], ld.at[9 + q]) for q in range(4)]
    local(down_w.at[:, cols(x)], wd.at[0], ld.at[8])

    route_weight(nb, 4, 1)

    for k in (1, 2, 3):
        got(ptb.at[4 - k], pt_r.at[0, 4 - k])
        got(ptf.at[4 - k], pt_r.at[1, 4 - k])

    yb_sends = [dispatch_half(0, xb, ptb, sbh, rbb, xb_r, yb_s, yb_r)]
    yb_sends.append(dispatch_half(1, xb, ptb, sbh, rbb, xb_r, yb_s, yb_r))
    for q in range(4):
        got(arr.at[q], pipe_r.at[1, q])
    rms_norm(arr, nf, None)
    nf_sends = spread_half(0, nf, xf, xf_s, xf_r) + spread_half(1, nf, xf, xf_s, xf_r)
    for q in range(4):
        got(inc.at[q], pipe_r.at[0, q])
    local(inc.at[x], xi.at[0], xi_r.at[0])
    for k in (1, 3, 2):
        post(inc.at[(x + k) % 4], xi.at[4 - k], xi_s.at[k], xi_r.at[4 - k], at_x(k))

    for c in load_beo:
        c.wait()

    def agree(i, _):
        r = pl.ds(pl.multiple_of(i * 16, 16), 16)
        total = jnp.zeros((16, 1), F32)
        for q in range(4):
            total += jnp.sum(inc[q, r, :].astype(F32) * beo[q, r, :].astype(F32), axis=1, keepdims=True)
        col[3, r, :] = jnp.broadcast_to(total, (16, 128))
        return 0

    lax.fori_loop(0, 4, agree, 0)

    route_weight(nf, 5, 2)

    got(rbb.at[0, 0], yb_r.at[0, 0])
    for c in yb_sends[0]:
        c.wait_send()
    sends += dispatch_half(0, xf, ptf, sbh, rbf, xf_r, yf_s, yf_r)

    got(rbb.at[1, 0], yb_r.at[0, 1])
    for c in yb_sends[1]:
        c.wait_send()
    sends += dispatch_half(1, xf, ptf, sbh, rbf, xf_r, yf_s, yf_r)

    for k in (1, 3, 2):
        post(down_w.at[:, cols((x + k) % 4)], wd.at[4 - k], wd_s.at[k], wd_r.at[4 - k], at_x(k))

    fill_i = place(lambda d: xi.at[d], ptb, sbi)

    def one_i(d, _):
        got(xi.at[d], xi_r.at[d])
        return fill_i(d, 0)

    lax.fori_loop(0, 4, one_i, 0)
    sends += to_experts(sbi, rbi, lambda o: yi_s.at[o], lambda o: yi_r.at[o])

    for i in range(2):
        for j in range(2):
            got(wn.at[j, i], w_r.at[j, i])
            got(wown.at[i, j], ld.at[4 + 2 * i + j])
    for j in range(2):
        for o in range(1, 8):
            got(rbb.at[j, o], yb_r.at[o, j])
    gate_up(rbb, 0)


    for j in range(2):
        for o in range(8):
            got(rbf.at[j, o], yf_r.at[o, j])
    gate_up(rbf, 1)
    for j in range(2):
        got(pr.at[1, j], rs_r.at[1, j])

    def act_f(m, _):
        r = pl.ds(pl.multiple_of(m * 32, 32), 32)
        g = acc[1, 0, r, :] + pr[1, 0, 0, r, :].astype(F32) + pr[1, 1, 0, r, :].astype(F32)
        u = acc[1, 1, r, :] + pr[1, 0, 1, r, :].astype(F32) + pr[1, 1, 1, r, :].astype(F32)
        hid[0, r, :] = (g * jax.nn.sigmoid(g) * u).astype(BF)
        return 0

    lax.fori_loop(0, ROWS // 32, act_f, 0)
    for k in (1, 3, 2):
        post(hid.at[0], hid.at[4 - k], hd_s.at[k], hd_r.at[4 - k], at_x(k))

    got(wd.at[0], ld.at[8])
    for d in (1, 2, 3):
        got(wd.at[d], wd_r.at[d])
    for o in range(8):
        got(rbi.at[o], yi_r.at[o])

    def back_own(m, _):
        r = pl.ds(pl.multiple_of(m * 256, 256), 256)
        bacc[r, :] = dot(rbi[pl.ds(m * 4, 4)].reshape(256, Q), wd[0], NT)
        return 0

    def back_other(n, _):
        d, m = 1 + n // 2, n % 2
        r = pl.ds(pl.multiple_of(m * 256, 256), 256)
        bs[d, r, :] = dot(rbi[pl.ds(m * 4, 4)].reshape(256, Q), wd[d], NT).astype(BF)
        return 0

    lax.fori_loop(0, 6, back_other, 0)
    for k in (1, 3, 2):
        post(bs.at[k], br.at[4 - k], bk_s.at[k], bk_r.at[4 - k], at_x(k))
    lax.fori_loop(0, 2, back_own, 0)

    for d in (1, 2, 3):
        got(hid.at[d], hd_r.at[d])

    def cols_f(n, _):
        c = pl.ds(pl.multiple_of(n * 256, 256), 256)
        r = dot(hid[0], wd[0, :, c])
        for d in (1, 2, 3):
            r += dot(hid[d], wd[d, :, c])
        rbi[:, :, c] = r.astype(BF).reshape(E, T, 256)
        return 0

    lax.fori_loop(0, Q // 256, cols_f, 0)
    back_home(rbi, rrf, lambda o: qf_s.at[o], lambda o: qf_r.at[o])

    for j in range(2):
        got(pr.at[0, j], rs_r.at[0, j])
    for d in (1, 2, 3):
        got(br.at[d], bk_r.at[d])

    def act_b(m, _):
        r = pl.ds(pl.multiple_of(m * 32, 32), 32)
        g = acc[0, 0, r, :] + pr[0, 0, 0, r, :].astype(F32) + pr[0, 1, 0, r, :].astype(F32)
        u = acc[0, 1, r, :] + pr[0, 0, 1, r, :].astype(F32) + pr[0, 1, 1, r, :].astype(F32)
        b = bacc[r, :] + br[1, r, :].astype(F32) + br[2, r, :].astype(F32) + br[3, r, :].astype(F32)
        s = jax.nn.sigmoid(g)
        dgu[0, r, :] = (b * u * s * (1.0 + g * (1.0 - s))).astype(BF)
        dgu[1, r, :] = (b * g * s).astype(BF)
        return 0

    lax.fori_loop(0, ROWS // 32, act_b, 0)
    post(dgu, dgn.at[0], dg_s.at[0], dg_r.at[0], at_x(off_a))
    post(dgu, dgn.at[1], dg_s.at[1], dg_r.at[1], at_x(off_b))

    input_part(1)
    for k in (1, 3, 2):
        post(rbb.at[1, :, slot_rows(k)], gb.at[4 - k], gb_s.at[k], gb_r.at[4 - k], at_x(k))
    input_part(0)
    back_home(rbb.at[0], rrb, lambda o: qb_s.at[o], lambda o: qb_r.at[o])

    for o in range(8):
        got(rrf.at[0], qf_r.at[o])
    unplace(rrf, ptf, lambda d: xi.at[d])
    for k in (1, 3, 2):
        post(xi.at[k], ff.at[4 - k], ff_s.at[k], ff_r.at[4 - k], at_x(k))

    for d in (1, 2, 3):
        got(gb.at[d], gb_r.at[d])

    def sum_b(o, _):
        own = rbb[1, o, slot_rows(0), :].astype(F32)
        gs[o, 0] = (own + gb[2, o].astype(F32)).astype(BF)
        gs[o, 1] = (gb[1, o].astype(F32) + gb[3, o].astype(F32)).astype(BF)
        return 0

    lax.fori_loop(0, E, sum_b, 0)
    back_home(gs, rrc, lambda o: qc_s.at[o], lambda o: qc_r.at[o])

    for o in range(8):
        got(rrb.at[0], qb_r.at[o])
    unplace(rrb, ptb, lambda d: xb.at[d, 0])
    for k in (1, 3, 2):
        post(xb.at[k, 0], fb.at[4 - k], fb_s.at[k], fb_r.at[4 - k], at_x(k))

    for c in nf_sends:
        c.wait_send()
    for d in (1, 2, 3):
        got(ff.at[d], ff_r.at[d])

    def finish_f(i, _):
        r = pl.ds(pl.multiple_of(i * 16, 16), 16)
        weight = col[2, r, 0:1]
        for d in range(4):
            q = (x + d) % 4
            e = (xi[0, r, :] if d == 0 else ff[d, r, :]).astype(F32)
            nf[q, r, :] = (arr[q, r, :].astype(F32) + SCALE * weight * e).astype(BF)
        return 0

    lax.fori_loop(0, 4, finish_f, 0)
    outs += [local(nf.at[q], fwd_out.at[:, pl.ds(q * Q, Q)], out_s.at[1, q]) for q in range(4)]

    for c in nb_sends:
        c.wait_send()
    for o in range(8):
        got(rrc.at[0], qc_r.at[o])
    for j in range(2):
        xb[j, 1] = dot(ptb[0], rrc[:, j].reshape(E * S, Q)).astype(BF)
    for d in (1, 2, 3):
        got(fb.at[d], fb_r.at[d])
    quarters = (
        (qa(x), lambda r: xb[0, 0, r, :].astype(F32) + fb[2, r, :].astype(F32)),
        (qa(x + 1), lambda r: fb[1, r, :].astype(F32) + fb[3, r, :].astype(F32)),
        (qb(x), lambda r: xb[0, 1, r, :].astype(F32)),
        (qb(x + 1), lambda r: xb[1, 1, r, :].astype(F32)),
    )

    def finish_b(i, _):
        r = pl.ds(pl.multiple_of(i * 16, 16), 16)
        inv = col[0, r, 0:1]
        weight = col[1, r, 0:1]
        d_logit = SCALE * col[3, r, 0:1] * weight * (1.0 - weight)
        hot = (lax.broadcasted_iota(jnp.int32, (16, E), 1).astype(F32) == col[4, r, 0:1]).astype(F32).astype(BF)
        total = jnp.zeros((16, 1), F32)
        for q, part in quarters:
            g = part(r)
            dn = SCALE * weight * g + d_logit * dot(hot, router_t[:, cols(q)])
            s = dn * gain[q]
            sg[q, r, :] = s
            total += jnp.sum(s * bi[q, r, :].astype(F32), axis=1, keepdims=True)
        factor = inv * inv * inv * (total * (1.0 / D))
        for q in range(4):
            v = bi[q, r, :].astype(F32)
            o = inc[q, r, :].astype(F32) + (inv * sg[q, r, :] - v * factor)
            nb[q, r, :] = o.astype(BF)
        return 0

    lax.fori_loop(0, 4, finish_b, 0)
    outs += [local(nb.at[q], bwd_out.at[:, pl.ds(q * Q, Q)], out_s.at[0, q]) for q in range(4)]

    for c in sends:
        c.wait_send()
    for c in outs:
        c.wait()


def hand_out(fwd_in, bwd_in, fwd_out, bwd_out):
    fwd_out[...] = fwd_in[...]
    bwd_out[...] = bwd_in[...]


def shards(
    fwd_src, fwd_route, bwd_input, bwd_expert_out, grad_src, bwd_route, norm_gain, router, gate_w, up_w, down_w
):
    hbm = pl.BlockSpec(memory_space=pl.ANY)
    vmem = pl.BlockSpec(memory_space=pltpu.VMEM)
    dma = pltpu.SemaphoreType.DMA

    def buf(*shape, dtype=BF):
        return pltpu.VMEM(shape, dtype)

    scratch = [
        buf(4, T, Q), buf(4, T, Q), buf(4, T, Q), buf(4, T, Q),
        buf(4, T, Q), buf(4, T, Q),
        buf(4, 2, T, Q), buf(4, 2, T, Q), buf(4, T, Q),
        buf(2, E, T, Q), buf(E, T, Q),
        buf(2, E, T, Q), buf(E, T, Q), buf(2, E, T, Q),
        buf(E, T, Q), buf(E, T, Q), buf(E, 2, S, Q),
        buf(4, E, S, Q), buf(E, 2, S, Q),
        buf(4, T, Q), buf(4, T, Q),
        buf(2, 2, Q, H), buf(2, 2, Q, H), buf(4, H, Q),
        buf(4, T, E * S), buf(4, T, E * S),
        buf(2, 2, ROWS, H, dtype=F32), buf(2, 2, 2, ROWS, H), buf(2, 2, 2, ROWS, H),
        buf(ROWS, H, dtype=F32), buf(4, ROWS, H), buf(4, ROWS, H),
        buf(2, ROWS, H), buf(2, 2, ROWS, H), buf(4, ROWS, H),
        buf(4, T, Q, dtype=F32), buf(6, T, 128, dtype=F32), buf(4, 1, Q, dtype=F32),
        dma((16,)), dma((2, 4)), dma((2, 4)), dma((2, 4)), dma((2, 4)),
        dma((2, 2)), dma((2, 2)), dma((4,)), dma((4,)),
        dma((4, 2)), dma((4, 2)), dma((4, 2)), dma((4, 2)), dma((4,)), dma((4,)),
        dma((8, 2)), dma((8, 2)), dma((8,)), dma((8,)), dma((8, 2)), dma((8, 2)),
        dma((2, 2)), dma((2, 2)), dma((4,)), dma((4,)), dma((2,)), dma((2,)), dma((4,)), dma((4,)),
        dma((4,)), dma((4,)), dma((8,)), dma((8,)), dma((8,)), dma((8,)), dma((8,)), dma((8,)),
        dma((4,)), dma((4,)), dma((4,)), dma((4,)), dma((2, 4)),
    ]
    out = jax.ShapeDtypeStruct((T, D), BF)
    fwd_out, bwd_out = pl.pallas_call(
        kernel,
        out_shape=(out, out),
        in_specs=[hbm, vmem, hbm, hbm, hbm, vmem, vmem, vmem, hbm, hbm, hbm],
        out_specs=(hbm, hbm),
        scratch_shapes=scratch,
        compiler_params=pltpu.CompilerParams(
            collective_id=0, has_side_effects=True, vmem_limit_bytes=62 * 1024 * 1024
        ),
        cost_estimate=pl.CostEstimate(
            flops=15_000_000_000, bytes_accessed=20_000_000, transcendentals=400_000
        ),
    )(
        fwd_src[0],
        fwd_route.reshape(1, T),
        bwd_input[0],
        bwd_expert_out[0],
        grad_src[0],
        bwd_route.reshape(1, T),
        norm_gain,
        router[0].T,
        gate_w[0].reshape(4, Q, H),
        up_w[0].reshape(4, Q, H),
        down_w[0],
    )
    rows = pl.BlockSpec((32, D), lambda i: (i, 0))
    fwd_out, bwd_out = pl.pallas_call(
        hand_out,
        out_shape=(out, out),
        grid=(2,),
        in_specs=[rows, rows],
        out_specs=(rows, rows),
    )(fwd_out, bwd_out)
    return (fwd_out[None], bwd_out[None])


def solution(mesh):
    placed = (
        P("pipe", "expert", None),
        P("pipe", "expert", None),
        P("pipe", "expert", None),
        P("pipe", "expert", None),
        P("pipe", "expert", None),
        P("pipe", "expert", None),
        P("pipe", None),
        P("pipe", None, None),
        P("pipe", None, "expert"),
        P("pipe", None, "expert"),
        P("pipe", "expert", None),
    )
    return jax.shard_map(
        shards,
        mesh=mesh,
        in_specs=placed,
        out_specs=(P("pipe", "expert", None), P("pipe", "expert", None)),
        check_vma=False,
    )
```
